32 devices in a mesh: param: 8 (over y, x, core), ex: 4 (over z).
Axes of the slice: x: 2, y: 2, z: 4, core: 2. Of those that a mesh axis runs over, the one named last changes fastest.
Arguments:
- activations: bfloat16 [4, 512, 8192], P('ex', None, 'param'), may hold values from -6 to 6
- cotangents: bfloat16 [4, 512, 1024], P('ex', 'param'), may hold values from -0.25 to 0.25
- signs: int32 [8388608], P('param'), may hold values from -1 to 1, as said below
- indices: int32 [32768], replicated, may hold values from 0 to 8388607
Outputs:
- projected: float32 [4, 32768], P('ex', 'param')
The draws below stay inside these ranges and needn't reach their ends.
Inputs may be any that keep to these rules, and one draw needn't show every extreme that they name: `signs`: every entry is -1 or +1.
All inputs are finite; a program needn't handle non-finite values.
Results may differ from the reference program's by a relative error of at most 0.0003.
Values may be sent and summed in bfloat16 or wider, within the bound.
No kernel may reach another device: no remote copies, remote signals or barrier semaphores. Data moves between devices by JAX's collectives and lax.ppermute only.
A program may use at most 64 MiB of HBM per device.

```python
import math
import jax
import jax.numpy as jnp
from jax import lax

DIN = 8192
DOUT = 1024
TOK = 512
SAMPLES = 32768
EXAMPLES = 4


def draw_signs(key, part):
    key = jax.random.fold_in(key, 7)
    return (2 * jax.random.randint(key, (DIN * DOUT,), 0, 2) - 1).astype(jnp.int32)


def touch_ends(entries, own_key, low, high):
    extent = entries.shape
    index_at = [jax.random.randint(jax.random.fold_in(own_key, axis), (), 0, extent[axis]) for axis in range(len(extent))]
    entries = entries.at[tuple(index_at)].set(low)
    longest = extent.index(max(extent))
    index_at[longest] = (index_at[longest] + 1) % extent[longest]
    return entries.at[tuple(index_at)].set(high)


def level_of(rng, shape, split, low, largest):
    gain, own = 1.0, jax.random.fold_in(rng, 6)
    for axis_at, parts in split:
        draws = jnp.exp(jax.random.uniform(jax.random.fold_in(own, axis_at), (parts,), jnp.float32, low / len(split), largest / len(split)))
        gain = gain * jnp.repeat(draws, shape[axis_at] // parts).reshape([-1 if axis == axis_at else 1 for axis in range(len(shape))])
    return gain


def normal_values(key, dims, scale, reach, pieces=(), held_as=jnp.bfloat16):
    entries = jax.random.normal(key, dims, jnp.float32) * scale
    if len(pieces) > 0:
        entries = level_of(key, dims, pieces, -0.22, 0.18) * entries
    return jnp.clip(entries, min=-reach, max=reach).astype(held_as)


def setup_inputs(seed: int = 0) -> dict:
    splits = jax.random.split(jax.random.key(seed), 5)
    activations = normal_values(splits[0], (EXAMPLES, TOK, DIN), 1.0, 6.0, ((0, 4), (2, 8)))
    cotangents = normal_values(splits[1], (EXAMPLES, TOK, DOUT), TOK ** -0.5, 0.25, ((0, 4), (1, 8)))
    signs = draw_signs(jax.random.fold_in(splits[4], 71), 0)
    indices = touch_ends(jax.random.randint(splits[3], (SAMPLES,), 0, DIN * DOUT), jax.random.fold_in(splits[3], 1), 0, (DIN * DOUT) - 1).astype(jnp.int32)
    return dict(activations=activations, cotangents=cotangents, signs=signs, indices=indices)


def walsh_last(values):
    leading = values.shape[:-1]
    length = values.shape[-1]
    stride = 1
    while stride < length:
        paired = values.reshape(leading + (length // (2 * stride), 2, stride))
        values = jnp.stack([paired[..., 0, :] + paired[..., 1, :], paired[..., 0, :] - paired[..., 1, :]], axis=-2).reshape(leading + (length,))
        stride = stride * 2
    return values

def reference(activations, cotangents, signs, indices):
    sign_matrix = signs.reshape(DIN, DOUT).astype(jnp.float32)
    scale_factor = 1.0 / math.sqrt(DIN * DOUT)

    def one_example(example_pair):
        inputs_here, grads_here = example_pair
        gradient = jnp.dot(inputs_here.T, grads_here, preferred_element_type=jnp.float32)
        signed = gradient * sign_matrix
        combined = walsh_last(signed)
        combined = walsh_last(combined.T).T
        return combined.reshape(-1)[indices] * scale_factor
    return lax.map(one_example, (activations, cotangents))
```

```python
import functools
import math

import jax
import jax.numpy as jnp
from jax import lax
from jax.experimental import pallas as pl
from jax.experimental.pallas import tpu as pltpu
from jax.sharding import PartitionSpec as P

LANES = 128
SIDE = 256


def flipped(x, axis, mask):
    return lax.ppermute(x, axis, [(i, i ^ mask) for i in range(lax.axis_size(axis))])


def parity(bits, width):
    shift = 1 << (width - 1).bit_length() >> 1
    while shift:
        bits = bits ^ (bits >> shift)
        shift //= 2
    return bits & 1


def butterfly(parts):
    stride = 1
    while stride < len(parts):
        parts = [
            parts[i] + parts[i + stride] if not i & stride else parts[i - stride] - parts[i]
            for i in range(len(parts))
        ]
        stride *= 2
    return parts


def split(x):
    high = x.astype(jnp.bfloat16)
    return high, (x - high.astype(jnp.float32)).astype(jnp.bfloat16)


def dot(left, right):
    return jnp.dot(left, right, preferred_element_type=jnp.float32)


def sketch_kernel(parties, scale, acts_ref, signs_ref, rows_ref, index_ref, *refs):
    chunk_refs, out_refs = refs[:parties], refs[parties : 2 * parties]
    cots, signed, table, picked, result = refs[2 * parties :]
    me = lax.axis_index("param")
    height = acts_ref.shape[0]
    breadth = signs_ref.shape[1]
    tokens = chunk_refs[0].shape[0]
    for distance in range(parties):
        start = pl.multiple_of((me ^ distance) * tokens, tokens)
        cots[pl.ds(start, tokens), :] = chunk_refs[distance][...]

    row_at = lax.broadcasted_iota(jnp.int32, (SIDE, SIDE), 0)
    col_at = lax.broadcasted_iota(jnp.int32, (SIDE, SIDE), 1)
    hadamard = (1 - 2 * parity(row_at & col_at, 8)).astype(jnp.float32).astype(jnp.bfloat16)

    row_blocks, col_blocks = height // SIDE, breadth // SIDE
    for col in range(col_blocks):
        cols = slice(col * SIDE, (col + 1) * SIDE)
        product = dot(acts_ref[...], cots[:, cols]) * signs_ref[:, cols].astype(jnp.float32)
        parts = butterfly([product[row * SIDE : (row + 1) * SIDE] for row in range(row_blocks)])
        for row in range(row_blocks):
            signed[row * SIDE : (row + 1) * SIDE, cols] = parts[row]
    for row in range(row_blocks):
        rows = slice(row * SIDE, (row + 1) * SIDE)
        parts = butterfly([signed[rows, col * SIDE : (col + 1) * SIDE] for col in range(col_blocks)])
        for col in range(col_blocks):
            high, low = split(parts[col])
            high, low = split(dot(high, hadamard) + dot(low, hadamard))
            done = dot(hadamard, high) + dot(hadamard, low)
            for piece in range(SIDE // LANES):
                at = (col * (SIDE // LANES) + piece) * height + row * SIDE
                table[at : at + SIDE, :] = done[:, piece * LANES : (piece + 1) * LANES]

    groups = index_ref.shape[0]
    sub_at = lax.broadcasted_iota(jnp.int32, (LANES, LANES), 0)

    def group(at, carry):
        for k in range(LANES):
            picked[k : k + 1, :] = table[pl.ds(rows_ref[at * LANES + k], 1), :]
        lane = index_ref[pl.ds(at, 1), :] & (LANES - 1)
        chosen = jnp.where(sub_at == lane, picked[...].T, 0.0)
        result[pl.ds(at, 1), :] = jnp.sum(chosen, axis=0, keepdims=True)
        return carry

    lax.fori_loop(0, groups, group, 0)

    share = groups // parties
    bits = (height * breadth).bit_length() - 1
    for distance in range(parties):
        at = pl.multiple_of((me ^ distance) * share, share)
        owner = index_ref[pl.ds(at, share), :] >> bits
        sign = (1 - 2 * parity(owner & me, parties.bit_length() - 1)).astype(jnp.float32)
        out_refs[distance][...] = result[pl.ds(at, share), :] * (sign * scale)


def on_device(activations, cotangents, signs, indices):
    height = activations.shape[2]
    breadth = cotangents.shape[2]
    parties = lax.axis_size("param")
    samples = indices.shape[0]
    groups = samples // LANES

    chunks = {0: cotangents[0]}
    for distance in range(2, parties, 2):
        chunks[distance] = flipped(chunks[0], "param", distance)
    for distance in range(0, parties, 2):
        chunks[distance + 1] = flipped(chunks[distance], "param", 1)

    acts = activations[0].T
    sign_matrix = signs.reshape(height, breadth).astype(jnp.bfloat16)
    offset = indices & (height * breadth - 1)
    rows = (offset // LANES) % (breadth // LANES) * height + offset // breadth
    vmem = pl.BlockSpec(memory_space=pltpu.VMEM)
    outs = pl.pallas_call(
        functools.partial(sketch_kernel, parties, 1.0 / math.sqrt(height * breadth * parties)),
        out_shape=[jax.ShapeDtypeStruct((groups // parties, LANES), jnp.float32)] * parties,
        in_specs=[vmem, vmem, pl.BlockSpec(memory_space=pltpu.SMEM), vmem] + [vmem] * parties,
        out_specs=[vmem] * parties,
        scratch_shapes=[
            pltpu.VMEM((activations.shape[1], breadth), jnp.bfloat16),
            pltpu.VMEM((height, breadth), jnp.float32),
            pltpu.VMEM((height * breadth // LANES, LANES), jnp.float32),
            pltpu.VMEM((LANES, LANES), jnp.float32),
            pltpu.VMEM((groups, LANES), jnp.float32),
        ],
        compiler_params=pltpu.CompilerParams(vmem_limit_bytes=40 * 1024 * 1024),
        name="sketch",
    )(acts, sign_matrix, rows, indices.reshape(groups, LANES), *[chunks[d] for d in range(parties)])

    total = outs[0]
    for distance in range(1, parties):
        total = total + flipped(outs[distance], "param", distance)
    return total.reshape(1, samples // parties)


def solution(mesh):
    in_specs = (P("ex", None, "param"), P("ex", "param", None), P("param"), P())
    out_specs = P("ex", "param")
    return jax.shard_map(
        on_device, mesh=mesh, in_specs=in_specs, out_specs=out_specs, check_vma=False
    )
```

```python
import functools
import math

import jax
import jax.numpy as jnp
from jax import lax
from jax.experimental import pallas as pl
from jax.experimental.pallas import tpu as pltpu
from jax.sharding import PartitionSpec as P

LANES = 128
SIDE = 256


def flipped(x, axis, mask):
    return lax.ppermute(x, axis, [(i, i ^ mask) for i in range(lax.axis_size(axis))])


def parity(bits, width):
    shift = 1 << (width - 1).bit_length() >> 1
    while shift:
        bits = bits ^ (bits >> shift)
        shift //= 2
    return bits & 1


def butterfly(parts):
    stride = 1
    while stride < len(parts):
        parts = [
            parts[i] + parts[i + stride] if not i & stride else parts[i - stride] - parts[i]
            for i in range(len(parts))
        ]
        stride *= 2
    return parts


def split(x):
    high = x.astype(jnp.bfloat16)
    return high, (x - high.astype(jnp.float32)).astype(jnp.bfloat16)


def dot(left, right):
    return jnp.dot(left, right, preferred_element_type=jnp.float32)


def transform_kernel(parties, acts_ref, signs_ref, *refs):
    chunk_refs = refs[:parties]
    table, cots, signed = refs[parties:]
    me = lax.axis_index("param")
    height = acts_ref.shape[0]
    breadth = signs_ref.shape[1]
    tokens = chunk_refs[0].shape[0]
    for distance in range(parties):
        start = pl.multiple_of((me ^ distance) * tokens, tokens)
        cots[pl.ds(start, tokens), :] = chunk_refs[distance][...]

    row_at = lax.broadcasted_iota(jnp.int32, (SIDE, SIDE), 0)
    col_at = lax.broadcasted_iota(jnp.int32, (SIDE, SIDE), 1)
    hadamard = (1 - 2 * parity(row_at & col_at, 8)).astype(jnp.float32).astype(jnp.bfloat16)

    row_blocks, col_blocks = height // SIDE, breadth // SIDE
    for col in range(col_blocks):
        cols = slice(col * SIDE, (col + 1) * SIDE)
        product = dot(acts_ref[...], cots[:, cols]) * signs_ref[:, cols].astype(jnp.float32)
        parts = butterfly([product[row * SIDE : (row + 1) * SIDE] for row in range(row_blocks)])
        for row in range(row_blocks):
            signed[row * SIDE : (row + 1) * SIDE, cols] = parts[row]
    for row in range(row_blocks):
        rows = slice(row * SIDE, (row + 1) * SIDE)
        parts = butterfly([signed[rows, col * SIDE : (col + 1) * SIDE] for col in range(col_blocks)])
        for col in range(col_blocks):
            high, low = split(parts[col])
            high, low = split(dot(high, hadamard) + dot(low, hadamard))
            done = dot(hadamard, high) + dot(hadamard, low)
            for piece in range(SIDE // LANES):
                at = (col * (SIDE // LANES) + piece) * height + row * SIDE
                table[at : at + SIDE, :] = done[:, piece * LANES : (piece + 1) * LANES]


def gather_kernel(parties, scale, table, rows_ref, index_ref, *refs):
    out_refs = refs[:parties]
    picked, result = refs[parties:]
    me = lax.axis_index("param")
    groups = index_ref.shape[0]
    sub_at = lax.broadcasted_iota(jnp.int32, (LANES, LANES), 0)

    def group(at, carry):
        for k in range(LANES):
            picked[k : k + 1, :] = table[rows_ref[at * LANES + k]]
        lane = index_ref[pl.ds(at, 1), :] & (LANES - 1)
        chosen = jnp.where(sub_at == lane, picked[...].T, 0.0)
        result[pl.ds(at, 1), :] = jnp.sum(chosen, axis=0, keepdims=True)
        return carry

    lax.fori_loop(0, groups, group, 0)

    share = groups // parties
    bits = (table.shape[0] * LANES).bit_length() - 1
    for distance in range(parties):
        at = pl.multiple_of((me ^ distance) * share, share)
        owner = index_ref[pl.ds(at, share), :] >> bits
        sign = (1 - 2 * parity(owner & me, parties.bit_length() - 1)).astype(jnp.float32)
        out_refs[distance][...] = result[pl.ds(at, share), :] * (sign * scale)


def on_device(activations, cotangents, signs, indices):
    height = activations.shape[2]
    breadth = cotangents.shape[2]
    parties = lax.axis_size("param")
    samples = indices.shape[0]
    groups = samples // LANES

    chunks = {0: cotangents[0]}
    for distance in range(2, parties, 2):
        chunks[distance] = flipped(chunks[0], "param", distance)
    for distance in range(0, parties, 2):
        chunks[distance + 1] = flipped(chunks[distance], "param", 1)

    acts = activations[0].T
    sign_matrix = signs.reshape(height, breadth).astype(jnp.bfloat16)
    offset = indices & (height * breadth - 1)
    rows = (offset // LANES) % (breadth // LANES) * height + offset // breadth
    vmem = pl.BlockSpec(memory_space=pltpu.VMEM)
    table_rows = height * breadth // LANES
    table = pl.pallas_call(
        functools.partial(transform_kernel, parties),
        out_shape=jax.ShapeDtypeStruct((table_rows, LANES), jnp.float32),
        in_specs=[vmem] * (2 + parties),
        out_specs=vmem,
        scratch_shapes=[
            pltpu.VMEM((activations.shape[1], breadth), jnp.bfloat16),
            pltpu.VMEM((height, breadth), jnp.float32),
        ],
        compiler_params=pltpu.CompilerParams(vmem_limit_bytes=32 * 1024 * 1024),
        name="transform",
    )(acts, sign_matrix, *[chunks[d] for d in range(parties)])
    outs = pl.pallas_call(
        functools.partial(gather_kernel, parties, 1.0 / math.sqrt(height * breadth * parties)),
        out_shape=[jax.ShapeDtypeStruct((groups // parties, LANES), jnp.float32)] * parties,
        in_specs=[vmem, pl.BlockSpec(memory_space=pltpu.SMEM), vmem],
        out_specs=[vmem] * parties,
        scratch_shapes=[
            pltpu.VMEM((LANES, LANES), jnp.float32),
            pltpu.VMEM((groups, LANES), jnp.float32),
        ],
        compiler_params=pltpu.CompilerParams(vmem_limit_bytes=32 * 1024 * 1024),
        name="gather",
    )(table.reshape(table_rows, 1, LANES), rows, indices.reshape(groups, LANES))

    total = outs[0]
    for distance in range(1, parties):
        total = total + flipped(outs[distance], "param", distance)
    return total.reshape(1, samples // parties)


def solution(mesh):
    in_specs = (P("ex", None, "param"), P("ex", "param", None), P("param"), P())
    out_specs = P("ex", "param")
    return jax.shard_map(
        on_device, mesh=mesh, in_specs=in_specs, out_specs=out_specs, check_vma=False
    )
```

```python
import functools
import math

import jax
import jax.numpy as jnp
from jax import lax
from jax.experimental import pallas as pl
from jax.experimental.pallas import tpu as pltpu
from jax.sharding import PartitionSpec as P

LANES = 128
SIDE = 256


def flipped(x, axis, mask):
    return lax.ppermute(x, axis, [(i, i ^ mask) for i in range(lax.axis_size(axis))])


def parity(bits, width):
    shift = 1 << (width - 1).bit_length() >> 1
    while shift:
        bits = bits ^ (bits >> shift)
        shift //= 2
    return bits & 1


def butterfly(parts):
    stride = 1
    while stride < len(parts):
        parts = [
            parts[i] + parts[i + stride] if not i & stride else parts[i - stride] - parts[i]
            for i in range(len(parts))
        ]
        stride *= 2
    return parts


def split(x):
    high = x.astype(jnp.bfloat16)
    return high, (x - high.astype(jnp.float32)).astype(jnp.bfloat16)


def dot(left, right):
    return jnp.dot(left, right, preferred_element_type=jnp.float32)


def transform_kernel(parties, acts_ref, signs_ref, *refs):
    chunk_refs = refs[:parties]
    table, cots, signed = refs[parties:]
    me = lax.axis_index("param")
    height = acts_ref.shape[0]
    breadth = signs_ref.shape[1]
    tokens = chunk_refs[0].shape[0]
    for distance in range(parties):
        start = pl.multiple_of((me ^ distance) * tokens, tokens)
        cots[pl.ds(start, tokens), :] = chunk_refs[distance][...]

    row_at = lax.broadcasted_iota(jnp.int32, (SIDE, SIDE), 0)
    col_at = lax.broadcasted_iota(jnp.int32, (SIDE, SIDE), 1)
    hadamard = (1 - 2 * parity(row_at & col_at, 8)).astype(jnp.float32).astype(jnp.bfloat16)

    row_blocks, col_blocks = height // SIDE, breadth // SIDE
    for col in range(col_blocks):
        cols = slice(col * SIDE, (col + 1) * SIDE)
        product = dot(acts_ref[...], cots[:, cols]) * signs_ref[:, cols].astype(jnp.float32)
        parts = butterfly([product[row * SIDE : (row + 1) * SIDE] for row in range(row_blocks)])
        for row in range(row_blocks):
            signed[row * SIDE : (row + 1) * SIDE, cols] = parts[row]
    for row in range(row_blocks):
        rows = slice(row * SIDE, (row + 1) * SIDE)
        parts = butterfly([signed[rows, col * SIDE : (col + 1) * SIDE] for col in range(col_blocks)])
        for col in range(col_blocks):
            high, low = split(parts[col])
            high, low = split(dot(high, hadamard) + dot(low, hadamard))
            done = dot(hadamard, high) + dot(hadamard, low)
            for piece in range(SIDE // LANES):
                at = (col * (SIDE // LANES) + piece) * height + row * SIDE
                table[at : at + SIDE, :] = done[:, piece * LANES : (piece + 1) * LANES]


def gather_kernel(parties, scale, table, rows_ref, index_ref, *refs):
    out_refs = refs[:parties]
    result, *picked = refs[parties:]
    me = lax.axis_index("param")
    groups = index_ref.shape[0]
    depth = len(picked)
    sub_at = lax.broadcasted_iota(jnp.int32, (LANES, LANES), 0)

    def choose(at, rows):
        lane = index_ref[pl.ds(at, 1), :] & (LANES - 1)
        chosen = jnp.where(sub_at == lane, rows[...].T, 0.0)
        result[pl.ds(at, 1), :] = jnp.sum(chosen, axis=0, keepdims=True)

    def step(at, carry):
        for slot in range(depth):
            group = at * depth + slot
            choose(jnp.maximum(group - 1, 0), picked[slot - 1])
            for k in range(LANES):
                picked[slot][k : k + 1, :] = table[rows_ref[group * LANES + k]]
        return carry

    lax.fori_loop(0, groups // depth, step, 0)
    choose(groups - 1, picked[-1])

    share = groups // parties
    bits = (table.shape[0] * LANES).bit_length() - 1
    for distance in range(parties):
        at = pl.multiple_of((me ^ distance) * share, share)
        owner = index_ref[pl.ds(at, share), :] >> bits
        sign = (1 - 2 * parity(owner & me, parties.bit_length() - 1)).astype(jnp.float32)
        out_refs[distance][...] = result[pl.ds(at, share), :] * (sign * scale)


def on_device(activations, cotangents, signs, indices):
    height = activations.shape[2]
    breadth = cotangents.shape[2]
    parties = lax.axis_size("param")
    samples = indices.shape[0]
    groups = samples // LANES

    chunks = {0: cotangents[0]}
    for distance in range(2, parties, 2):
        chunks[distance] = flipped(chunks[0], "param", distance)
    for distance in range(0, parties, 2):
        chunks[distance + 1] = flipped(chunks[distance], "param", 1)

    acts = activations[0].T
    sign_matrix = signs.reshape(height, breadth).astype(jnp.bfloat16)
    offset = indices & (height * breadth - 1)
    rows = (offset // LANES) % (breadth // LANES) * height + offset // breadth
    vmem = pl.BlockSpec(memory_space=pltpu.VMEM)
    table_rows = height * breadth // LANES
    table = pl.pallas_call(
        functools.partial(transform_kernel, parties),
        out_shape=jax.ShapeDtypeStruct((table_rows, LANES), jnp.float32),
        in_specs=[vmem] * (2 + parties),
        out_specs=vmem,
        scratch_shapes=[
            pltpu.VMEM((activations.shape[1], breadth), jnp.bfloat16),
            pltpu.VMEM((height, breadth), jnp.float32),
        ],
        compiler_params=pltpu.CompilerParams(vmem_limit_bytes=32 * 1024 * 1024),
        name="transform",
    )(acts, sign_matrix, *[chunks[d] for d in range(parties)])
    outs = pl.pallas_call(
        functools.partial(gather_kernel, parties, 1.0 / math.sqrt(height * breadth * parties)),
        out_shape=[jax.ShapeDtypeStruct((groups // parties, LANES), jnp.float32)] * parties,
        in_specs=[vmem, pl.BlockSpec(memory_space=pltpu.SMEM), vmem],
        out_specs=[vmem] * parties,
        scratch_shapes=[pltpu.VMEM((groups, LANES), jnp.float32)]
        + [pltpu.VMEM((LANES, LANES), jnp.float32)] * 4,
        compiler_params=pltpu.CompilerParams(vmem_limit_bytes=32 * 1024 * 1024),
        name="gather",
    )(table.reshape(table_rows, 1, LANES), rows, indices.reshape(groups, LANES))

    total = outs[0]
    for distance in range(1, parties):
        total = total + flipped(outs[distance], "param", distance)
    return total.reshape(1, samples // parties)


def solution(mesh):
    in_specs = (P("ex", None, "param"), P("ex", "param", None), P("param"), P())
    out_specs = P("ex", "param")
    return jax.shard_map(
        on_device, mesh=mesh, in_specs=in_specs, out_specs=out_specs, check_vma=False
    )
```

```python
import functools
import math

import jax
import jax.numpy as jnp
from jax import lax
from jax.experimental import pallas as pl
from jax.experimental.pallas import tpu as pltpu
from jax.sharding import PartitionSpec as P

LANES = 128
SIDE = 256


def flipped(x, axis, mask):
    return lax.ppermute(x, axis, [(i, i ^ mask) for i in range(lax.axis_size(axis))])


def parity(bits, width):
    shift = 1 << (width - 1).bit_length() >> 1
    while shift:
        bits = bits ^ (bits >> shift)
        shift //= 2
    return bits & 1


def butterfly(parts):
    stride = 1
    while stride < len(parts):
        parts = [
            parts[i] + parts[i + stride] if not i & stride else parts[i - stride] - parts[i]
            for i in range(len(parts))
        ]
        stride *= 2
    return parts


def split(x):
    high = x.astype(jnp.bfloat16)
    return high, (x - high.astype(jnp.float32)).astype(jnp.bfloat16)


def dot(left, right):
    return jnp.dot(left, right, preferred_element_type=jnp.float32)


def transform_kernel(parties, acts_ref, signs_ref, *refs):
    chunk_refs = refs[:parties]
    table, cots, signed = refs[parties:]
    me = lax.axis_index("param")
    height = acts_ref.shape[0]
    breadth = signs_ref.shape[1]
    tokens = chunk_refs[0].shape[0]
    for distance in range(parties):
        start = pl.multiple_of((me ^ distance) * tokens, tokens)
        cots[pl.ds(start, tokens), :] = chunk_refs[distance][...]

    row_at = lax.broadcasted_iota(jnp.int32, (SIDE, SIDE), 0)
    col_at = lax.broadcasted_iota(jnp.int32, (SIDE, SIDE), 1)
    hadamard = (1 - 2 * parity(row_at & col_at, 8)).astype(jnp.float32).astype(jnp.bfloat16)

    row_blocks, col_blocks = height // SIDE, breadth // SIDE
    for col in range(col_blocks):
        cols = slice(col * SIDE, (col + 1) * SIDE)
        product = dot(acts_ref[...], cots[:, cols]) * signs_ref[:, cols].astype(jnp.float32)
        parts = butterfly([product[row * SIDE : (row + 1) * SIDE] for row in range(row_blocks)])
        for row in range(row_blocks):
            signed[row * SIDE : (row + 1) * SIDE, cols] = parts[row]
    for row in range(row_blocks):
        rows = slice(row * SIDE, (row + 1) * SIDE)
        parts = butterfly([signed[rows, col * SIDE : (col + 1) * SIDE] for col in range(col_blocks)])
        for col in range(col_blocks):
            high, low = split(parts[col])
            high, low = split(dot(high, hadamard) + dot(low, hadamard))
            done = dot(hadamard, high) + dot(hadamard, low)
            for piece in range(SIDE // LANES):
                at = (col * (SIDE // LANES) + piece) * height + row * SIDE
                table[at : at + SIDE, :] = done[:, piece * LANES : (piece + 1) * LANES]


def gather_kernel(parties, scale, table, rows_ref, index_ref, *refs):
    out_refs = refs[:parties]
    result, *picked = refs[parties:]
    me = lax.axis_index("param")
    groups = index_ref.shape[0]
    depth = len(picked)
    sub_at = lax.broadcasted_iota(jnp.int32, (LANES, LANES), 0)

    def choose(at, rows):
        lane = index_ref[pl.ds(at, 1), :] & (LANES - 1)
        chosen = jnp.where(sub_at == lane, rows[...].T, 0.0)
        result[pl.ds(at, 1), :] = jnp.sum(chosen, axis=0, keepdims=True)

    def step(at, carry):
        for slot in range(depth):
            group = at * depth + slot
            choose(jnp.maximum(group - 1, 0), picked[slot - 1])
            single = picked[slot].reshape(LANES, 1, LANES)
            for k in range(LANES):
                single[k] = table[rows_ref[group * LANES + k]]
        return carry

    lax.fori_loop(0, groups // depth, step, 0)
    choose(groups - 1, picked[-1])

    share = groups // parties
    bits = (table.shape[0] * LANES).bit_length() - 1
    for distance in range(parties):
        at = pl.multiple_of((me ^ distance) * share, share)
        owner = index_ref[pl.ds(at, share), :] >> bits
        sign = (1 - 2 * parity(owner & me, parties.bit_length() - 1)).astype(jnp.float32)
        out_refs[distance][...] = result[pl.ds(at, share), :] * (sign * scale)


def on_device(activations, cotangents, signs, indices):
    height = activations.shape[2]
    breadth = cotangents.shape[2]
    parties = lax.axis_size("param")
    samples = indices.shape[0]
    groups = samples // LANES

    chunks = {0: cotangents[0]}
    for distance in range(2, parties, 2):
        chunks[distance] = flipped(chunks[0], "param", distance)
    for distance in range(0, parties, 2):
        chunks[distance + 1] = flipped(chunks[distance], "param", 1)

    acts = activations[0].T
    sign_matrix = signs.reshape(height, breadth).astype(jnp.bfloat16)
    offset = indices & (height * breadth - 1)
    rows = (offset // LANES) % (breadth // LANES) * height + offset // breadth
    vmem = pl.BlockSpec(memory_space=pltpu.VMEM)
    table_rows = height * breadth // LANES
    table = pl.pallas_call(
        functools.partial(transform_kernel, parties),
        out_shape=jax.ShapeDtypeStruct((table_rows, LANES), jnp.float32),
        in_specs=[vmem] * (2 + parties),
        out_specs=vmem,
        scratch_shapes=[
            pltpu.VMEM((activations.shape[1], breadth), jnp.bfloat16),
            pltpu.VMEM((height, breadth), jnp.float32),
        ],
        compiler_params=pltpu.CompilerParams(vmem_limit_bytes=32 * 1024 * 1024),
        name="transform",
    )(acts, sign_matrix, *[chunks[d] for d in range(parties)])
    outs = pl.pallas_call(
        functools.partial(gather_kernel, parties, 1.0 / math.sqrt(height * breadth * parties)),
        out_shape=[jax.ShapeDtypeStruct((groups // parties, LANES), jnp.float32)] * parties,
        in_specs=[vmem, pl.BlockSpec(memory_space=pltpu.SMEM), vmem],
        out_specs=[vmem] * parties,
        scratch_shapes=[pltpu.VMEM((groups, LANES), jnp.float32)]
        + [pltpu.VMEM((LANES, LANES), jnp.float32)] * 4,
        compiler_params=pltpu.CompilerParams(vmem_limit_bytes=32 * 1024 * 1024),
        name="gather",
    )(table.reshape(table_rows, 1, LANES), rows, indices.reshape(groups, LANES))

    total = outs[0]
    for distance in range(1, parties):
        total = total + flipped(outs[distance], "param", distance)
    return total.reshape(1, samples // parties)


def solution(mesh):
    in_specs = (P("ex", None, "param"), P("ex", "param", None), P("param"), P())
    out_specs = P("ex", "param")
    return jax.shard_map(
        on_device, mesh=mesh, in_specs=in_specs, out_specs=out_specs, check_vma=False
    )
```

```python
import functools
import math

import jax
import jax.numpy as jnp
from jax import lax
from jax.experimental import pallas as pl
from jax.experimental.pallas import tpu as pltpu
from jax.sharding import PartitionSpec as P

LANES = 128
SIDE = 256
BATCH = 16


def flipped(x, axis, mask):
    return lax.ppermute(x, axis, [(i, i ^ mask) for i in range(lax.axis_size(axis))])


def parity(bits, width):
    shift = 1 << (width - 1).bit_length() >> 1
    while shift:
        bits = bits ^ (bits >> shift)
        shift //= 2
    return bits & 1


def butterfly(parts):
    stride = 1
    while stride < len(parts):
        parts = [
            parts[i] + parts[i + stride] if not i & stride else parts[i - stride] - parts[i]
            for i in range(len(parts))
        ]
        stride *= 2
    return parts


def split(x):
    high = x.astype(jnp.bfloat16)
    return high, (x - high.astype(jnp.float32)).astype(jnp.bfloat16)


def dot(left, right):
    return jnp.dot(left, right, preferred_element_type=jnp.float32)


def transform_kernel(parties, acts_ref, signs_ref, *refs):
    chunk_refs = refs[:parties]
    table, cots, signed = refs[parties:]
    me = lax.axis_index("param")
    height = acts_ref.shape[0]
    breadth = signs_ref.shape[1]
    tokens = chunk_refs[0].shape[0]
    for distance in range(parties):
        start = pl.multiple_of((me ^ distance) * tokens, tokens)
        cots[pl.ds(start, tokens), :] = chunk_refs[distance][...]

    row_at = lax.broadcasted_iota(jnp.int32, (SIDE, SIDE), 0)
    col_at = lax.broadcasted_iota(jnp.int32, (SIDE, SIDE), 1)
    hadamard = (1 - 2 * parity(row_at & col_at, 8)).astype(jnp.float32).astype(jnp.bfloat16)

    row_blocks, col_blocks = height // SIDE, breadth // SIDE
    for col in range(col_blocks):
        cols = slice(col * SIDE, (col + 1) * SIDE)
        product = dot(acts_ref[...], cots[:, cols]) * signs_ref[:, cols].astype(jnp.float32)
        parts = butterfly([product[row * SIDE : (row + 1) * SIDE] for row in range(row_blocks)])
        for row in range(row_blocks):
            signed[row * SIDE : (row + 1) * SIDE, cols] = parts[row]
    for row in range(row_blocks):
        rows = slice(row * SIDE, (row + 1) * SIDE)
        parts = butterfly([signed[rows, col * SIDE : (col + 1) * SIDE] for col in range(col_blocks)])
        for col in range(col_blocks):
            high, low = split(parts[col])
            high, low = split(dot(high, hadamard) + dot(low, hadamard))
            done = dot(hadamard, high) + dot(hadamard, low)
            for piece in range(SIDE // LANES):
                at = (col * (SIDE // LANES) + piece) * height + row * SIDE
                table[at : at + SIDE, :] = done[:, piece * LANES : (piece + 1) * LANES]


def gather_kernel(parties, scale, table, rows_ref, index_ref, *refs):
    out_refs = refs[:parties]
    result, *picked = refs[parties:]
    me = lax.axis_index("param")
    groups = index_ref.shape[0]
    depth = len(picked)
    sub_at = lax.broadcasted_iota(jnp.int32, (LANES, LANES), 0)

    def choose(at, rows):
        lane = index_ref[pl.ds(at, 1), :] & (LANES - 1)
        chosen = jnp.where(sub_at == lane, rows[...].T, 0.0)
        result[pl.ds(at, 1), :] = jnp.sum(chosen, axis=0, keepdims=True)

    def step(at, carry):
        for slot in range(depth):
            group = at * depth + slot
            choose(jnp.maximum(group - 1, 0), picked[slot - 1])
            single = picked[slot].reshape(LANES, 1, LANES)
            for first in range(0, LANES, BATCH):
                rows = [table[rows_ref[group * LANES + first + k]] for k in range(BATCH)]
                for k in range(BATCH):
                    single[first + k] = rows[k]
        return carry

    lax.fori_loop(0, groups // depth, step, 0)
    choose(groups - 1, picked[-1])

    share = groups // parties
    bits = (table.shape[0] * LANES).bit_length() - 1
    for distance in range(parties):
        at = pl.multiple_of((me ^ distance) * share, share)
        owner = index_ref[pl.ds(at, share), :] >> bits
        sign = (1 - 2 * parity(owner & me, parties.bit_length() - 1)).astype(jnp.float32)
        out_refs[distance][...] = result[pl.ds(at, share), :] * (sign * scale)


def on_device(activations, cotangents, signs, indices):
    height = activations.shape[2]
    breadth = cotangents.shape[2]
    parties = lax.axis_size("param")
    samples = indices.shape[0]
    groups = samples // LANES

    chunks = {0: cotangents[0]}
    for distance in range(2, parties, 2):
        chunks[distance] = flipped(chunks[0], "param", distance)
    for distance in range(0, parties, 2):
        chunks[distance + 1] = flipped(chunks[distance], "param", 1)

    acts = activations[0].T
    sign_matrix = signs.reshape(height, breadth).astype(jnp.bfloat16)
    offset = indices & (height * breadth - 1)
    rows = (offset // LANES) % (breadth // LANES) * height + offset // breadth
    vmem = pl.BlockSpec(memory_space=pltpu.VMEM)
    table_rows = height * breadth // LANES
    table = pl.pallas_call(
        functools.partial(transform_kernel, parties),
        out_shape=jax.ShapeDtypeStruct((table_rows, LANES), jnp.float32),
        in_specs=[vmem] * (2 + parties),
        out_specs=vmem,
        scratch_shapes=[
            pltpu.VMEM((activations.shape[1], breadth), jnp.bfloat16),
            pltpu.VMEM((height, breadth), jnp.float32),
        ],
        compiler_params=pltpu.CompilerParams(vmem_limit_bytes=32 * 1024 * 1024),
        name="transform",
    )(acts, sign_matrix, *[chunks[d] for d in range(parties)])
    outs = pl.pallas_call(
        functools.partial(gather_kernel, parties, 1.0 / math.sqrt(height * breadth * parties)),
        out_shape=[jax.ShapeDtypeStruct((groups // parties, LANES), jnp.float32)] * parties,
        in_specs=[vmem, pl.BlockSpec(memory_space=pltpu.SMEM), vmem],
        out_specs=[vmem] * parties,
        scratch_shapes=[pltpu.VMEM((groups, LANES), jnp.float32)]
        + [pltpu.VMEM((LANES, LANES), jnp.float32)] * 4,
        compiler_params=pltpu.CompilerParams(vmem_limit_bytes=32 * 1024 * 1024),
        name="gather",
    )(table.reshape(table_rows, 1, LANES), rows, indices.reshape(groups, LANES))

    total = outs[0]
    for distance in range(1, parties):
        total = total + flipped(outs[distance], "param", distance)
    return total.reshape(1, samples // parties)


def solution(mesh):
    in_specs = (P("ex", None, "param"), P("ex", "param", None), P("param"), P())
    out_specs = P("ex", "param")
    return jax.shard_map(
        on_device, mesh=mesh, in_specs=in_specs, out_specs=out_specs, check_vma=False
    )
```

```python
import functools
import math

import jax
import jax.numpy as jnp
from jax import lax
from jax.experimental import pallas as pl
from jax.experimental.pallas import tpu as pltpu
from jax.sharding import PartitionSpec as P

LANES = 128
SIDE = 256
BATCH = 16


def flipped(x, axis, mask):
    return lax.ppermute(x, axis, [(i, i ^ mask) for i in range(lax.axis_size(axis))])


def parity(bits, width):
    shift = 1 << (width - 1).bit_length() >> 1
    while shift:
        bits = bits ^ (bits >> shift)
        shift //= 2
    return bits & 1


def butterfly(parts):
    stride = 1
    while stride < len(parts):
        parts = [
            parts[i] + parts[i + stride] if not i & stride else parts[i - stride] - parts[i]
            for i in range(len(parts))
        ]
        stride *= 2
    return parts


def split(x):
    high = x.astype(jnp.bfloat16)
    return high, (x - high.astype(jnp.float32)).astype(jnp.bfloat16)


def dot(left, right):
    return jnp.dot(left, right, preferred_element_type=jnp.float32)


def transform_kernel(parties, acts_ref, signs_ref, *refs):
    chunk_refs = refs[:parties]
    table, cots, signed = refs[parties:]
    me = lax.axis_index("param")
    height = acts_ref.shape[0]
    breadth = signs_ref.shape[1]
    tokens = chunk_refs[0].shape[0]
    for distance in range(parties):
        start = pl.multiple_of((me ^ distance) * tokens, tokens)
        cots[pl.ds(start, tokens), :] = chunk_refs[distance][...]

    row_at = lax.broadcasted_iota(jnp.int32, (SIDE, SIDE), 0)
    col_at = lax.broadcasted_iota(jnp.int32, (SIDE, SIDE), 1)
    hadamard = (1 - 2 * parity(row_at & col_at, 8)).astype(jnp.float32).astype(jnp.bfloat16)

    row_blocks, col_blocks = height // SIDE, breadth // SIDE
    for col in range(col_blocks):
        cols = slice(col * SIDE, (col + 1) * SIDE)
        product = dot(acts_ref[...], cots[:, cols]) * signs_ref[:, cols].astype(jnp.float32)
        parts = butterfly([product[row * SIDE : (row + 1) * SIDE] for row in range(row_blocks)])
        for row in range(row_blocks):
            signed[row * SIDE : (row + 1) * SIDE, cols] = parts[row]
    for row in range(row_blocks):
        rows = slice(row * SIDE, (row + 1) * SIDE)
        parts = butterfly([signed[rows, col * SIDE : (col + 1) * SIDE] for col in range(col_blocks)])
        for col in range(col_blocks):
            high, low = split(parts[col])
            high, low = split(dot(high, hadamard) + dot(low, hadamard))
            done = dot(hadamard, high) + dot(hadamard, low)
            for piece in range(SIDE // LANES):
                at = (col * (SIDE // LANES) + piece) * height + row * SIDE
                table[at : at + SIDE, :] = done[:, piece * LANES : (piece + 1) * LANES]


def gather_kernel(parties, scale, table, rows_ref, index_ref, *refs):
    out_refs = refs[:parties]
    result, *picked = refs[parties:]
    me = lax.axis_index("param")
    groups = index_ref.shape[0]
    depth = len(picked)
    sub_at = lax.broadcasted_iota(jnp.int32, (LANES, LANES), 0)
    diagonal = sub_at == lax.broadcasted_iota(jnp.int32, (LANES, LANES), 1)

    def choose(at, rows):
        lane = index_ref[pl.ds(at, 1), :] & (LANES - 1)
        mask = jnp.where(sub_at == lane, 1.0, 0.0).astype(jnp.bfloat16)
        both = jnp.concatenate(split(rows[...]), axis=1)
        pairs = dot(both, jnp.concatenate([mask, mask], axis=0))
        result[pl.ds(at, 1), :] = jnp.sum(jnp.where(diagonal, pairs, 0.0), axis=0, keepdims=True)

    def step(at, carry):
        for slot in range(depth):
            group = at * depth + slot
            choose(jnp.maximum(group - 1, 0), picked[slot - 1])
            single = picked[slot].reshape(LANES, 1, LANES)
            for first in range(0, LANES, BATCH):
                rows = [table[rows_ref[group * LANES + first + k]] for k in range(BATCH)]
                for k in range(BATCH):
                    single[first + k] = rows[k]
        return carry

    lax.fori_loop(0, groups // depth, step, 0)
    choose(groups - 1, picked[-1])

    share = groups // parties
    bits = (table.shape[0] * LANES).bit_length() - 1
    for distance in range(parties):
        at = pl.multiple_of((me ^ distance) * share, share)
        owner = index_ref[pl.ds(at, share), :] >> bits
        sign = (1 - 2 * parity(owner & me, parties.bit_length() - 1)).astype(jnp.float32)
        out_refs[distance][...] = result[pl.ds(at, share), :] * (sign * scale)


def on_device(activations, cotangents, signs, indices):
    height = activations.shape[2]
    breadth = cotangents.shape[2]
    parties = lax.axis_size("param")
    samples = indices.shape[0]
    groups = samples // LANES

    chunks = {0: cotangents[0]}
    for distance in range(2, parties, 2):
        chunks[distance] = flipped(chunks[0], "param", distance)
    for distance in range(0, parties, 2):
        chunks[distance + 1] = flipped(chunks[distance], "param", 1)

    acts = activations[0].T
    sign_matrix = signs.reshape(height, breadth).astype(jnp.bfloat16)
    offset = indices & (height * breadth - 1)
    rows = (offset // LANES) % (breadth // LANES) * height + offset // breadth
    vmem = pl.BlockSpec(memory_space=pltpu.VMEM)
    table_rows = height * breadth // LANES
    table = pl.pallas_call(
        functools.partial(transform_kernel, parties),
        out_shape=jax.ShapeDtypeStruct((table_rows, LANES), jnp.float32),
        in_specs=[vmem] * (2 + parties),
        out_specs=vmem,
        scratch_shapes=[
            pltpu.VMEM((activations.shape[1], breadth), jnp.bfloat16),
            pltpu.VMEM((height, breadth), jnp.float32),
        ],
        compiler_params=pltpu.CompilerParams(vmem_limit_bytes=32 * 1024 * 1024),
        name="transform",
    )(acts, sign_matrix, *[chunks[d] for d in range(parties)])
    outs = pl.pallas_call(
        functools.partial(gather_kernel, parties, 1.0 / math.sqrt(height * breadth * parties)),
        out_shape=[jax.ShapeDtypeStruct((groups // parties, LANES), jnp.float32)] * parties,
        in_specs=[vmem, pl.BlockSpec(memory_space=pltpu.SMEM), vmem],
        out_specs=[vmem] * parties,
        scratch_shapes=[pltpu.VMEM((groups, LANES), jnp.float32)]
        + [pltpu.VMEM((LANES, LANES), jnp.float32)] * 4,
        compiler_params=pltpu.CompilerParams(vmem_limit_bytes=32 * 1024 * 1024),
        name="gather",
    )(table.reshape(table_rows, 1, LANES), rows, indices.reshape(groups, LANES))

    total = outs[0]
    for distance in range(1, parties):
        total = total + flipped(outs[distance], "param", distance)
    return total.reshape(1, samples // parties)


def solution(mesh):
    in_specs = (P("ex", None, "param"), P("ex", "param", None), P("param"), P())
    out_specs = P("ex", "param")
    return jax.shard_map(
        on_device, mesh=mesh, in_specs=in_specs, out_specs=out_specs, check_vma=False
    )
```

```python
import functools
import math

import jax
import jax.numpy as jnp
from jax import lax
from jax.experimental import pallas as pl
from jax.experimental.pallas import tpu as pltpu
from jax.sharding import PartitionSpec as P

LANES = 128
SIDE = 256
SUBLANES = 8


def flipped(x, axis, mask):
    return lax.ppermute(x, axis, [(i, i ^ mask) for i in range(lax.axis_size(axis))])


def parity(bits, width):
    shift = 1 << (width - 1).bit_length() >> 1
    while shift:
        bits = bits ^ (bits >> shift)
        shift //= 2
    return bits & 1


def butterfly(parts):
    stride = 1
    while stride < len(parts):
        parts = [
            parts[i] + parts[i + stride] if not i & stride else parts[i - stride] - parts[i]
            for i in range(len(parts))
        ]
        stride *= 2
    return parts


def split(x):
    high = x.astype(jnp.bfloat16)
    return high, (x - high.astype(jnp.float32)).astype(jnp.bfloat16)


def dot(left, right):
    return jnp.dot(left, right, preferred_element_type=jnp.float32)


def transform_kernel(parties, acts_ref, signs_ref, *refs):
    chunk_refs = refs[:parties]
    table, cots, signed = refs[parties:]
    me = lax.axis_index("param")
    height = acts_ref.shape[0]
    breadth = signs_ref.shape[1]
    tokens = chunk_refs[0].shape[0]
    for distance in range(parties):
        start = pl.multiple_of((me ^ distance) * tokens, tokens)
        cots[pl.ds(start, tokens), :] = chunk_refs[distance][...]

    row_at = lax.broadcasted_iota(jnp.int32, (SIDE, SIDE), 0)
    col_at = lax.broadcasted_iota(jnp.int32, (SIDE, SIDE), 1)
    hadamard = (1 - 2 * parity(row_at & col_at, 8)).astype(jnp.float32).astype(jnp.bfloat16)

    row_blocks, col_blocks = height // SIDE, breadth // SIDE
    for col in range(col_blocks):
        cols = slice(col * SIDE, (col + 1) * SIDE)
        product = dot(acts_ref[...], cots[:, cols]) * signs_ref[:, cols].astype(jnp.float32)
        parts = butterfly([product[row * SIDE : (row + 1) * SIDE] for row in range(row_blocks)])
        for row in range(row_blocks):
            signed[row * SIDE : (row + 1) * SIDE, cols] = parts[row]
    for row in range(row_blocks):
        rows = slice(row * SIDE, (row + 1) * SIDE)
        parts = butterfly([signed[rows, col * SIDE : (col + 1) * SIDE] for col in range(col_blocks)])
        for col in range(col_blocks):
            high, low = split(parts[col])
            high, low = split(dot(high, hadamard) + dot(low, hadamard))
            done = dot(hadamard, high) + dot(hadamard, low)
            for piece in range(SIDE // LANES):
                at = (col * (SIDE // LANES) + piece) * height + row * SIDE
                table[at : at + SIDE, :] = done[:, piece * LANES : (piece + 1) * LANES]


def gather_kernel(parties, scale, table, rows_ref, index_ref, *refs):
    out_refs = refs[:parties]
    result, *picked = refs[parties:]
    me = lax.axis_index("param")
    groups = index_ref.shape[0]
    depth = len(picked)
    sub_at = lax.broadcasted_iota(jnp.int32, (LANES, LANES), 0)

    def choose(at, rows):
        lane = index_ref[pl.ds(at, 1), :] & (LANES - 1)
        chosen = jnp.where(sub_at == lane, rows[...].T, 0.0)
        result[pl.ds(at, 1), :] = jnp.sum(chosen, axis=0, keepdims=True)

    def step(at, carry):
        for slot in range(depth):
            group = at * depth + slot
            choose(jnp.maximum(group - 1, 0), picked[slot - 1])
            for first in range(0, LANES, SUBLANES):
                at_rows = [rows_ref[group * LANES + first + k] for k in range(SUBLANES)]
                copies = [table[pl.ds(row, SUBLANES, stride=0), :] for row in at_rows]
                merged = copies[0]
                for k in range(1, SUBLANES):
                    merged = jnp.where(sub_at[:SUBLANES] == k, copies[k], merged)
                picked[slot][first : first + SUBLANES, :] = merged
        return carry

    lax.fori_loop(0, groups // depth, step, 0)
    choose(groups - 1, picked[-1])

    share = groups // parties
    bits = ((table.shape[0] - SUBLANES) * LANES).bit_length() - 1
    for distance in range(parties):
        at = pl.multiple_of((me ^ distance) * share, share)
        owner = index_ref[pl.ds(at, share), :] >> bits
        sign = (1 - 2 * parity(owner & me, parties.bit_length() - 1)).astype(jnp.float32)
        out_refs[distance][...] = result[pl.ds(at, share), :] * (sign * scale)


def on_device(activations, cotangents, signs, indices):
    height = activations.shape[2]
    breadth = cotangents.shape[2]
    parties = lax.axis_size("param")
    samples = indices.shape[0]
    groups = samples // LANES

    chunks = {0: cotangents[0]}
    for distance in range(2, parties, 2):
        chunks[distance] = flipped(chunks[0], "param", distance)
    for distance in range(0, parties, 2):
        chunks[distance + 1] = flipped(chunks[distance], "param", 1)

    acts = activations[0].T
    sign_matrix = signs.reshape(height, breadth).astype(jnp.bfloat16)
    offset = indices & (height * breadth - 1)
    rows = (offset // LANES) % (breadth // LANES) * height + offset // breadth
    vmem = pl.BlockSpec(memory_space=pltpu.VMEM)
    table_rows = height * breadth // LANES
    table = pl.pallas_call(
        functools.partial(transform_kernel, parties),
        out_shape=jax.ShapeDtypeStruct((table_rows + SUBLANES, LANES), jnp.float32),
        in_specs=[vmem] * (2 + parties),
        out_specs=vmem,
        scratch_shapes=[
            pltpu.VMEM((activations.shape[1], breadth), jnp.bfloat16),
            pltpu.VMEM((height, breadth), jnp.float32),
        ],
        compiler_params=pltpu.CompilerParams(vmem_limit_bytes=32 * 1024 * 1024),
        name="transform",
    )(acts, sign_matrix, *[chunks[d] for d in range(parties)])
    outs = pl.pallas_call(
        functools.partial(gather_kernel, parties, 1.0 / math.sqrt(height * breadth * parties)),
        out_shape=[jax.ShapeDtypeStruct((groups // parties, LANES), jnp.float32)] * parties,
        in_specs=[vmem, pl.BlockSpec(memory_space=pltpu.SMEM), vmem],
        out_specs=[vmem] * parties,
        scratch_shapes=[pltpu.VMEM((groups, LANES), jnp.float32)]
        + [pltpu.VMEM((LANES, LANES), jnp.float32)] * 4,
        compiler_params=pltpu.CompilerParams(vmem_limit_bytes=32 * 1024 * 1024),
        name="gather",
    )(table, rows, indices.reshape(groups, LANES))

    total = outs[0]
    for distance in range(1, parties):
        total = total + flipped(outs[distance], "param", distance)
    return total.reshape(1, samples // parties)


def solution(mesh):
    in_specs = (P("ex", None, "param"), P("ex", "param", None), P("param"), P())
    out_specs = P("ex", "param")
    return jax.shard_map(
        on_device, mesh=mesh, in_specs=in_specs, out_specs=out_specs, check_vma=False
    )
```

```python
import functools
import math

import jax
import jax.numpy as jnp
from jax import lax
from jax.experimental import pallas as pl
from jax.experimental.pallas import tpu as pltpu
from jax.sharding import PartitionSpec as P

LANES = 128
SIDE = 256
SUBLANES = 8
LIMIT = 32 * 1024 * 1024


def flipped(x, axis, mask):
    return lax.ppermute(x, axis, [(i, i ^ mask) for i in range(lax.axis_size(axis))])


def parity(bits, width):
    shift = 1 << (width - 1).bit_length() >> 1
    while shift:
        bits = bits ^ (bits >> shift)
        shift //= 2
    return bits & 1


def butterfly(parts):
    stride = 1
    while stride < len(parts):
        parts = [
            parts[i] + parts[i + stride] if not i & stride else parts[i - stride] - parts[i]
            for i in range(len(parts))
        ]
        stride *= 2
    return parts


def split(x):
    high = x.astype(jnp.bfloat16)
    return high, (x - high.astype(jnp.float32)).astype(jnp.bfloat16)


def dot(left, right):
    return jnp.dot(left, right, preferred_element_type=jnp.float32)


def prepare_kernel(breadth, acts_ref, signs_ref, index_ref, packed_ref, rows_ref):
    spread = breadth // LANES
    rows = packed_ref.shape[0]
    for piece in range(spread):
        part = signs_ref[pl.ds(piece, rows, stride=spread), :]
        packed_ref[:, piece * LANES : (piece + 1) * LANES] = part.astype(jnp.float32).astype(jnp.bfloat16)
    packed_ref[:, breadth:] = acts_ref[...].T
    height = rows * pl.num_programs(0)
    index = index_ref[...]
    at_row = (index // LANES) % spread * height + index // breadth % height
    half = index // (breadth * height) % 2
    rows_ref[...] = half * (spread * height) + at_row


def transform_kernel(parties, own_ref, other_ref, *refs):
    chunk_refs = refs[:parties]
    table, cots, total, change = refs[parties:]
    me = lax.axis_index("param")
    height, breadth = total.shape
    tokens = chunk_refs[0].shape[0]
    for distance in range(parties):
        start = pl.multiple_of((me ^ distance) * tokens, tokens)
        cots[pl.ds(start, tokens), :] = chunk_refs[distance][...]

    row_at = lax.broadcasted_iota(jnp.int32, (SIDE, SIDE), 0)
    col_at = lax.broadcasted_iota(jnp.int32, (SIDE, SIDE), 1)
    hadamard = (1 - 2 * parity(row_at & col_at, 8)).astype(jnp.float32).astype(jnp.bfloat16)

    row_blocks, col_blocks = height // SIDE, breadth // SIDE
    for col in range(col_blocks):
        cols = slice(col * SIDE, (col + 1) * SIDE)
        own, other = [
            dot(ref[:, breadth:], cots[:, cols]) * ref[:, cols].astype(jnp.float32)
            for ref in (own_ref, other_ref)
        ]
        for signed, product in ((total, own + other), (change, own - other)):
            parts = butterfly([product[row * SIDE : (row + 1) * SIDE] for row in range(row_blocks)])
            for row in range(row_blocks):
                signed[row * SIDE : (row + 1) * SIDE, cols] = parts[row]
    for half, signed in enumerate((total, change)):
        for row in range(row_blocks):
            rows = slice(row * SIDE, (row + 1) * SIDE)
            parts = butterfly([signed[rows, col * SIDE : (col + 1) * SIDE] for col in range(col_blocks)])
            for col in range(col_blocks):
                high, low = split(parts[col])
                high, low = split(dot(high, hadamard) + dot(low, hadamard))
                done = dot(hadamard, high) + dot(hadamard, low)
                for piece in range(SIDE // LANES):
                    at = (half * (breadth // LANES) + col * (SIDE // LANES) + piece) * height + row * SIDE
                    table[at : at + SIDE, :] = done[:, piece * LANES : (piece + 1) * LANES]


def gather_kernel(parties, scale, table, rows_ref, index_ref, *refs):
    out_refs = refs[: parties // 2]
    result, *picked = refs[parties // 2 :]
    me = lax.axis_index("param")
    share = index_ref.shape[0] // parties
    groups = share * len(out_refs)
    depth = len(picked)
    sub_at = lax.broadcasted_iota(jnp.int32, (LANES, LANES), 0)

    def place(group):
        return (me ^ (group // share * 2)) * share + group % share

    def choose(group, rows):
        lane = index_ref[pl.ds(place(group), 1), :] & (LANES - 1)
        chosen = jnp.where(sub_at == lane, rows[...].T, 0.0)
        result[pl.ds(group, 1), :] = jnp.sum(chosen, axis=0, keepdims=True)

    def step(at, carry):
        for slot in range(depth):
            group = at * depth + slot
            choose(jnp.maximum(group - 1, 0), picked[slot - 1])
            base = place(group) * LANES
            for first in range(0, LANES, SUBLANES):
                at_rows = [rows_ref[base + first + k] for k in range(SUBLANES)]
                copies = [table[pl.ds(row, SUBLANES, stride=0), :] for row in at_rows]
                merged = copies[0]
                for k in range(1, SUBLANES):
                    merged = jnp.where(sub_at[:SUBLANES] == k, copies[k], merged)
                picked[slot][first : first + SUBLANES, :] = merged
        return carry

    lax.fori_loop(0, groups // depth, step, 0)
    choose(groups - 1, picked[-1])

    bits = ((table.shape[0] - SUBLANES) // 2 * LANES).bit_length() - 1
    for step_at, out_ref in enumerate(out_refs):
        at = pl.multiple_of((me ^ (2 * step_at)) * share, share)
        owner = index_ref[pl.ds(at, share), :] >> bits
        sign = (1 - 2 * parity(owner & me, parties.bit_length() - 1)).astype(jnp.float32)
        out_ref[...] = result[step_at * share : (step_at + 1) * share, :] * (sign * scale)


def on_device(activations, cotangents, signs, indices):
    tokens, height = activations.shape[1:]
    breadth = cotangents.shape[2]
    parties = lax.axis_size("param")
    samples = indices.shape[0]
    groups = samples // LANES
    table_rows = height * breadth // LANES
    vmem = pl.BlockSpec(memory_space=pltpu.VMEM)
    limit = pltpu.CompilerParams(vmem_limit_bytes=LIMIT)

    chunks = {0: cotangents[0]}
    for distance in range(2, parties, 2):
        chunks[distance] = flipped(chunks[0], "param", distance)

    steps = height // LANES
    packed, rows = pl.pallas_call(
        functools.partial(prepare_kernel, breadth),
        grid=(steps,),
        out_shape=[
            jax.ShapeDtypeStruct((height, breadth + tokens), jnp.bfloat16),
            jax.ShapeDtypeStruct((groups, LANES), jnp.int32),
        ],
        in_specs=[
            pl.BlockSpec((tokens, LANES), lambda at: (0, at)),
            pl.BlockSpec((table_rows // steps, LANES), lambda at: (at, 0)),
            pl.BlockSpec((groups // steps, LANES), lambda at: (at, 0)),
        ],
        out_specs=[
            pl.BlockSpec((LANES, breadth + tokens), lambda at: (at, 0)),
            pl.BlockSpec((groups // steps, LANES), lambda at: (at, 0)),
        ],
        compiler_params=limit,
        name="prepare",
    )(activations[0], signs.reshape(table_rows, LANES), indices.reshape(groups, LANES))
    other = flipped(packed, "param", 1)

    for distance in range(0, parties, 2):
        chunks[distance + 1] = flipped(chunks[distance], "param", 1)

    table = pl.pallas_call(
        functools.partial(transform_kernel, parties),
        out_shape=jax.ShapeDtypeStruct((2 * table_rows + SUBLANES, LANES), jnp.float32),
        in_specs=[vmem] * (2 + parties),
        out_specs=vmem,
        scratch_shapes=[
            pltpu.VMEM((tokens, breadth), jnp.bfloat16),
            pltpu.VMEM((height, breadth), jnp.float32),
            pltpu.VMEM((height, breadth), jnp.float32),
        ],
        compiler_params=limit,
        name="transform",
    )(packed, other, *[chunks[d] for d in range(parties)])
    outs = pl.pallas_call(
        functools.partial(gather_kernel, parties, 1.0 / math.sqrt(height * breadth * parties)),
        out_shape=[jax.ShapeDtypeStruct((groups // parties, LANES), jnp.float32)] * (parties // 2),
        in_specs=[vmem, pl.BlockSpec(memory_space=pltpu.SMEM), vmem],
        out_specs=[vmem] * (parties // 2),
        scratch_shapes=[pltpu.VMEM((groups // 2, LANES), jnp.float32)]
        + [pltpu.VMEM((LANES, LANES), jnp.float32)] * 4,
        compiler_params=limit,
        name="gather",
    )(table, rows.reshape(samples), indices.reshape(groups, LANES))

    total = outs[0]
    for step_at in range(1, parties // 2):
        total = total + flipped(outs[step_at], "param", 2 * step_at)
    return total.reshape(1, samples // parties)


def solution(mesh):
    in_specs = (P("ex", None, "param"), P("ex", "param", None), P("param"), P())
    out_specs = P("ex", "param")
    return jax.shard_map(
        on_device, mesh=mesh, in_specs=in_specs, out_specs=out_specs, check_vma=False
    )
```

```python
import functools
import math

import jax
import jax.numpy as jnp
from jax import lax
from jax.experimental import pallas as pl
from jax.experimental.pallas import tpu as pltpu
from jax.sharding import PartitionSpec as P

LANES = 128
LANE_BITS = 7
SIDE = 256
SUBLANES = 8
LIMIT = 40 * 1024 * 1024


def flipped(x, axis, mask):
    return lax.ppermute(x, axis, [(i, i ^ mask) for i in range(lax.axis_size(axis))])


def parity(bits, width):
    shift = 1 << (width - 1).bit_length() >> 1
    while shift:
        bits = bits ^ (bits >> shift)
        shift //= 2
    return bits & 1


def butterfly(parts):
    stride = 1
    while stride < len(parts):
        parts = [
            parts[i] + parts[i + stride] if not i & stride else parts[i - stride] - parts[i]
            for i in range(len(parts))
        ]
        stride *= 2
    return parts


def split(x):
    high = x.astype(jnp.bfloat16)
    return high, (x - high.astype(jnp.float32)).astype(jnp.bfloat16)


def dot(left, right):
    return jnp.dot(left, right, preferred_element_type=jnp.float32)


def prepare_kernel(acts_ref, signs_ref, index_ref, turned_ref, signs_out_ref, rows_ref):
    rows, breadth = signs_out_ref.shape
    spread = breadth // LANES
    for piece in range(spread):
        part = signs_ref[pl.ds(piece, rows, stride=spread), :]
        signs_out_ref[:, piece * LANES : (piece + 1) * LANES] = part.astype(jnp.float32).astype(jnp.bfloat16)
    turned_ref[...] = acts_ref[...].T
    height = rows * pl.num_programs(0)
    index = index_ref[...]
    at_row = ((index >> LANE_BITS) & (spread - 1)) * height + ((index // breadth) & (height - 1))
    half = (index // (breadth * height)) & 1
    rows_ref[...] = half * (spread * height) + at_row


def sketch_kernel(parties, scale, own_turned, own_signs, other_acts, other_signs, index_ref, rows_hbm, *refs):
    outs = parties // 2
    chunk_refs, out_refs, scratch = refs[:parties], refs[parties : parties + outs], refs[parties + outs :]
    table, cots, other_turned, total, change, result, rows_ref, rows_sems, *picked = scratch
    me = lax.axis_index("param")
    height, breadth = total.shape
    spread = breadth // LANES
    tokens = chunk_refs[0].shape[0]
    share = index_ref.shape[0] // parties

    def index_of(out):
        return index_ref[pl.ds(pl.multiple_of((me ^ (2 * out)) * share, share), share), :]

    copies = []
    for out in range(outs):
        source = rows_hbm.at[pl.ds(pl.multiple_of((me ^ (2 * out)) * share, share), share), :]
        target = rows_ref.at[pl.ds(out * share, share), :]
        copies.append(pltpu.make_async_copy(source, target, rows_sems.at[out]))
    for copy in copies:
        copy.start()

    for distance in range(parties):
        start = pl.multiple_of((me ^ distance) * tokens, tokens)
        cots[pl.ds(start, tokens), :] = chunk_refs[distance][...]
    other_turned[...] = other_acts[...].T

    row_at = lax.broadcasted_iota(jnp.int32, (SIDE, SIDE), 0)
    col_at = lax.broadcasted_iota(jnp.int32, (SIDE, SIDE), 1)
    hadamard = (1 - 2 * parity(row_at & col_at, 8)).astype(jnp.float32).astype(jnp.bfloat16)

    row_blocks, col_blocks, pieces = height // SIDE, breadth // SIDE, SIDE // LANES
    for col in range(col_blocks):
        cols = slice(col * SIDE, (col + 1) * SIDE)
        own = dot(own_turned[...], cots[:, cols]) * own_signs[:, cols].astype(jnp.float32)
        strips = [other_signs[pl.ds(col * pieces + piece, height, stride=spread), :] for piece in range(pieces)]
        other = dot(other_turned[...], cots[:, cols]) * jnp.concatenate(strips, axis=1).astype(jnp.float32)
        for signed, product in ((total, own + other), (change, own - other)):
            parts = butterfly([product[row * SIDE : (row + 1) * SIDE] for row in range(row_blocks)])
            for row in range(row_blocks):
                signed[row * SIDE : (row + 1) * SIDE, cols] = parts[row]
    for half, signed in enumerate((total, change)):
        for row in range(row_blocks):
            rows = slice(row * SIDE, (row + 1) * SIDE)
            parts = butterfly([signed[rows, col * SIDE : (col + 1) * SIDE] for col in range(col_blocks)])
            for col in range(col_blocks):
                high, low = split(parts[col])
                high, low = split(dot(high, hadamard) + dot(low, hadamard))
                done = dot(hadamard, high) + dot(hadamard, low)
                for piece in range(pieces):
                    at = (half * spread + col * pieces + piece) * height + row * SIDE
                    table[at : at + SIDE, :] = done[:, piece * LANES : (piece + 1) * LANES]

    for copy in copies:
        copy.wait()
    groups = share * outs
    depth = len(picked)
    sub_at = lax.broadcasted_iota(jnp.int32, (LANES, LANES), 0)

    def choose(group, rows):
        place = (me ^ (group // share * 2)) * share + group % share
        lane = index_ref[pl.ds(place, 1), :] & (LANES - 1)
        chosen = jnp.where(sub_at == lane, rows[...].T, 0.0)
        result[pl.ds(group, 1), :] = jnp.sum(chosen, axis=0, keepdims=True)

    def step(at, carry):
        for slot in range(depth):
            group = at * depth + slot
            choose(jnp.maximum(group - 1, 0), picked[slot - 1])
            for first in range(0, LANES, SUBLANES):
                at_rows = [rows_ref[group, first + k] for k in range(SUBLANES)]
                lines = [table[pl.ds(row, SUBLANES, stride=0), :] for row in at_rows]
                merged = lines[0]
                for k in range(1, SUBLANES):
                    merged = jnp.where(sub_at[:SUBLANES] == k, lines[k], merged)
                picked[slot][first : first + SUBLANES, :] = merged
        return carry

    lax.fori_loop(0, groups // depth, step, 0)
    choose(groups - 1, picked[-1])

    bits = (height * breadth).bit_length() - 1
    for out, out_ref in enumerate(out_refs):
        sign = (1 - 2 * parity((index_of(out) >> bits) & me, parties.bit_length() - 1)).astype(jnp.float32)
        out_ref[...] = result[out * share : (out + 1) * share, :] * (sign * scale)


def on_device(activations, cotangents, signs, indices):
    tokens, height = activations.shape[1:]
    breadth = cotangents.shape[2]
    parties = lax.axis_size("param")
    samples = indices.shape[0]
    groups = samples // LANES
    table_rows = height * breadth // LANES
    outs = parties // 2
    vmem = pl.BlockSpec(memory_space=pltpu.VMEM)

    chunks = {0: cotangents[0]}
    for distance in range(2, parties, 2):
        chunks[distance] = flipped(chunks[0], "param", distance)
    for distance in range(0, parties, 2):
        chunks[distance + 1] = flipped(chunks[distance], "param", 1)
    acts = activations[0]
    sign_rows = signs.reshape(table_rows, LANES)
    index_rows = indices.reshape(groups, LANES)
    other_acts, other_signs = flipped(acts, "param", 1), flipped(sign_rows, "param", 1)

    steps = height // LANES
    turned, sign_matrix, rows = pl.pallas_call(
        prepare_kernel,
        grid=(steps,),
        out_shape=[
            jax.ShapeDtypeStruct((height, tokens), jnp.bfloat16),
            jax.ShapeDtypeStruct((height, breadth), jnp.bfloat16),
            jax.ShapeDtypeStruct((groups, LANES), jnp.int32),
        ],
        in_specs=[
            pl.BlockSpec((tokens, LANES), lambda at: (0, at)),
            pl.BlockSpec((table_rows // steps, LANES), lambda at: (at, 0)),
            pl.BlockSpec((groups // steps, LANES), lambda at: (at, 0)),
        ],
        out_specs=[
            pl.BlockSpec((LANES, tokens), lambda at: (at, 0)),
            pl.BlockSpec((LANES, breadth), lambda at: (at, 0)),
            pl.BlockSpec((groups // steps, LANES), lambda at: (at, 0)),
        ],
        compiler_params=pltpu.CompilerParams(vmem_limit_bytes=LIMIT),
        cost_estimate=pl.CostEstimate(flops=0, bytes_accessed=8 * height * breadth, transcendentals=0),
        name="prepare",
    )(acts, sign_rows, index_rows)

    sums = pl.pallas_call(
        functools.partial(sketch_kernel, parties, 1.0 / math.sqrt(height * breadth * parties)),
        out_shape=[jax.ShapeDtypeStruct((groups // parties, LANES), jnp.float32)] * outs,
        in_specs=[vmem] * 5 + [pl.BlockSpec(memory_space=pl.ANY)] + [vmem] * parties,
        out_specs=[vmem] * outs,
        scratch_shapes=[
            pltpu.VMEM((2 * table_rows + SUBLANES, LANES), jnp.float32),
            pltpu.VMEM((tokens, breadth), jnp.bfloat16),
            pltpu.VMEM((height, tokens), jnp.bfloat16),
            pltpu.VMEM((height, breadth), jnp.float32),
            pltpu.VMEM((height, breadth), jnp.float32),
            pltpu.VMEM((groups // 2, LANES), jnp.float32),
            pltpu.SMEM((groups // 2, LANES), jnp.int32),
            pltpu.SemaphoreType.DMA((outs,)),
        ]
        + [pltpu.VMEM((LANES, LANES), jnp.float32)] * 4,
        compiler_params=pltpu.CompilerParams(vmem_limit_bytes=LIMIT),
        name="sketch",
    )(
        turned,
        sign_matrix,
        other_acts,
        other_signs,
        index_rows,
        rows,
        *[chunks[d] for d in range(parties)],
    )

    total = sums[0]
    for out in range(1, outs):
        total = total + flipped(sums[out], "param", 2 * out)
    return total.reshape(1, samples // parties)


def solution(mesh):
    in_specs = (P("ex", None, "param"), P("ex", "param", None), P("param"), P())
    out_specs = P("ex", "param")
    return jax.shard_map(
        on_device, mesh=mesh, in_specs=in_specs, out_specs=out_specs, check_vma=False
    )
```

```python
import functools
import math

import jax
import jax.numpy as jnp
from jax import lax
from jax.experimental import pallas as pl
from jax.experimental.pallas import tpu as pltpu
from jax.sharding import PartitionSpec as P

LANES = 128
LANE_BITS = 7
SIDE = 256
SUBLANES = 8
LIMIT = 40 * 1024 * 1024


def flipped(x, axis, mask):
    return lax.ppermute(x, axis, [(i, i ^ mask) for i in range(lax.axis_size(axis))])


def parity(bits, width):
    shift = 1 << (width - 1).bit_length() >> 1
    while shift:
        bits = bits ^ (bits >> shift)
        shift //= 2
    return bits & 1


def butterfly(parts):
    stride = 1
    while stride < len(parts):
        parts = [
            parts[i] + parts[i + stride] if not i & stride else parts[i - stride] - parts[i]
            for i in range(len(parts))
        ]
        stride *= 2
    return parts


def split(x):
    high = x.astype(jnp.bfloat16)
    return high, (x - high.astype(jnp.float32)).astype(jnp.bfloat16)


def dot(left, right):
    return jnp.dot(left, right, preferred_element_type=jnp.float32)


def sketch_kernel(parties, scale, index_hbm, own_cots_hbm, own_acts_hbm, own_signs_hbm, other_acts, other_signs, *refs):
    outs = parties // 2
    chunk_refs, out_refs, scratch = refs[: parties - 1], refs[parties - 1 : parties - 1 + outs], refs[parties - 1 + outs :]
    index_ref, own_acts, own_signs, in_sems, *scratch = scratch
    table, cots, turned, total, change, result, rows_vmem, rows_ref, rows_sem, *picked = scratch
    me = lax.axis_index("param")
    height, breadth = total.shape
    spread = breadth // LANES
    tokens = chunk_refs[0].shape[0]
    share = index_ref.shape[0] // parties
    own_start = pl.multiple_of(me * tokens, tokens)
    loads = [
        pltpu.make_async_copy(source, target, in_sems.at[at])
        for at, (source, target) in enumerate(
            (
                (index_hbm, index_ref),
                (own_cots_hbm, cots.at[pl.ds(own_start, tokens), :]),
                (own_acts_hbm, own_acts),
                (own_signs_hbm, own_signs),
            )
        )
    ]
    for load in loads:
        load.start()

    def index_of(out):
        return index_ref[pl.ds(pl.multiple_of((me ^ (2 * out)) * share, share), share), :]

    for distance in range(1, parties):
        start = pl.multiple_of((me ^ distance) * tokens, tokens)
        cots[pl.ds(start, tokens), :] = chunk_refs[distance - 1][...]
    turned[1] = other_acts[...].T

    loads[0].wait()
    for out in range(outs):
        index = index_of(out)
        at_row = ((index >> LANE_BITS) & (spread - 1)) * height + ((index // breadth) & (height - 1))
        half = (index // (breadth * height)) & 1
        rows_vmem[out * share : (out + 1) * share, :] = half * (spread * height) + at_row
    copy = pltpu.make_async_copy(rows_vmem, rows_ref, rows_sem)
    copy.start()

    loads[1].wait()
    loads[2].wait()
    turned[0] = own_acts[...].T
    loads[3].wait()

    row_at = lax.broadcasted_iota(jnp.int32, (SIDE, SIDE), 0)
    col_at = lax.broadcasted_iota(jnp.int32, (SIDE, SIDE), 1)
    hadamard = (1 - 2 * parity(row_at & col_at, 8)).astype(jnp.float32).astype(jnp.bfloat16)

    row_blocks, col_blocks, pieces = height // SIDE, breadth // SIDE, SIDE // LANES
    for col in range(col_blocks):
        cols = slice(col * SIDE, (col + 1) * SIDE)
        products = []
        for side, signs in enumerate((own_signs, other_signs)):
            strips = [signs[pl.ds(col * pieces + piece, height, stride=spread), :] for piece in range(pieces)]
            sign = jnp.concatenate(strips, axis=1).astype(jnp.float32)
            products.append(dot(turned[side], cots[:, cols]) * sign)
        own, other = products
        for signed, product in ((total, own + other), (change, own - other)):
            parts = butterfly([product[row * SIDE : (row + 1) * SIDE] for row in range(row_blocks)])
            for row in range(row_blocks):
                signed[row * SIDE : (row + 1) * SIDE, cols] = parts[row]
    for half, signed in enumerate((total, change)):
        for row in range(row_blocks):
            rows = slice(row * SIDE, (row + 1) * SIDE)
            parts = butterfly([signed[rows, col * SIDE : (col + 1) * SIDE] for col in range(col_blocks)])
            for col in range(col_blocks):
                high, low = split(parts[col])
                high, low = split(dot(high, hadamard) + dot(low, hadamard))
                done = dot(hadamard, high) + dot(hadamard, low)
                for piece in range(pieces):
                    at = (half * spread + col * pieces + piece) * height + row * SIDE
                    table[at : at + SIDE, :] = done[:, piece * LANES : (piece + 1) * LANES]

    copy.wait()
    groups = share * outs
    depth = len(picked)
    sub_at = lax.broadcasted_iota(jnp.int32, (LANES, LANES), 0)

    def choose(group, rows):
        place = (me ^ (group // share * 2)) * share + group % share
        lane = index_ref[pl.ds(place, 1), :] & (LANES - 1)
        chosen = jnp.where(sub_at == lane, rows[...].T, 0.0)
        result[pl.ds(group, 1), :] = jnp.sum(chosen, axis=0, keepdims=True)

    def step(at, carry):
        for slot in range(depth):
            group = at * depth + slot
            choose(jnp.maximum(group - 1, 0), picked[slot - 1])
            for first in range(0, LANES, SUBLANES):
                at_rows = [rows_ref[group, first + k] for k in range(SUBLANES)]
                copies = [table[pl.ds(row, SUBLANES, stride=0), :] for row in at_rows]
                merged = copies[0]
                for k in range(1, SUBLANES):
                    merged = jnp.where(sub_at[:SUBLANES] == k, copies[k], merged)
                picked[slot][first : first + SUBLANES, :] = merged
        return carry

    lax.fori_loop(0, groups // depth, step, 0)
    choose(groups - 1, picked[-1])

    bits = (height * breadth).bit_length() - 1
    for out, out_ref in enumerate(out_refs):
        sign = (1 - 2 * parity((index_of(out) >> bits) & me, parties.bit_length() - 1)).astype(jnp.float32)
        out_ref[...] = result[out * share : (out + 1) * share, :] * (sign * scale)


def on_device(activations, cotangents, signs, indices):
    tokens, height = activations.shape[1:]
    breadth = cotangents.shape[2]
    parties = lax.axis_size("param")
    samples = indices.shape[0]
    groups = samples // LANES
    table_rows = height * breadth // LANES
    outs = parties // 2
    vmem = pl.BlockSpec(memory_space=pltpu.VMEM)

    chunks = {0: cotangents[0]}
    for distance in range(2, parties, 2):
        chunks[distance] = flipped(chunks[0], "param", distance)
    for distance in range(0, parties, 2):
        chunks[distance + 1] = flipped(chunks[distance], "param", 1)
    acts = activations[0]
    sign_rows = signs.reshape(table_rows, LANES)

    sums = pl.pallas_call(
        functools.partial(sketch_kernel, parties, 1.0 / math.sqrt(height * breadth * parties)),
        out_shape=[jax.ShapeDtypeStruct((groups // parties, LANES), jnp.float32)] * outs,
        in_specs=[pl.BlockSpec(memory_space=pltpu.HBM)] * 4 + [vmem] * (1 + parties),
        out_specs=[vmem] * outs,
        scratch_shapes=[
            pltpu.VMEM((groups, LANES), jnp.int32),
            pltpu.VMEM((tokens, height), jnp.bfloat16),
            pltpu.VMEM((table_rows, LANES), jnp.int32),
            pltpu.SemaphoreType.DMA((4,)),
            pltpu.VMEM((2 * table_rows + SUBLANES, LANES), jnp.float32),
            pltpu.VMEM((tokens, breadth), jnp.bfloat16),
            pltpu.VMEM((2, height, tokens), jnp.bfloat16),
            pltpu.VMEM((height, breadth), jnp.float32),
            pltpu.VMEM((height, breadth), jnp.float32),
            pltpu.VMEM((groups // 2, LANES), jnp.float32),
            pltpu.VMEM((groups // 2, LANES), jnp.int32),
            pltpu.SMEM((groups // 2, LANES), jnp.int32),
            pltpu.SemaphoreType.DMA,
        ]
        + [pltpu.VMEM((LANES, LANES), jnp.float32)] * 4,
        compiler_params=pltpu.CompilerParams(vmem_limit_bytes=LIMIT),
        name="sketch",
    )(
        *[
            pltpu.with_memory_space_constraint(x, pltpu.HBM)
            for x in (indices.reshape(groups, LANES), chunks[0], acts, sign_rows)
        ],
        flipped(acts, "param", 1),
        flipped(sign_rows, "param", 1),
        *[chunks[d] for d in range(1, parties)],
    )

    total = sums[0]
    for out in range(1, outs):
        total = total + flipped(sums[out], "param", 2 * out)
    return total.reshape(1, samples // parties)


def solution(mesh):
    in_specs = (P("ex", None, "param"), P("ex", "param", None), P("param"), P())
    out_specs = P("ex", "param")
    return jax.shard_map(
        on_device, mesh=mesh, in_specs=in_specs, out_specs=out_specs, check_vma=False
    )
```

```python
import functools
import math

import jax
import jax.numpy as jnp
from jax import lax
from jax.experimental import pallas as pl
from jax.experimental.pallas import tpu as pltpu
from jax.sharding import PartitionSpec as P

LANES = 128
LANE_BITS = 7
SIDE = 256
SUBLANES = 8
LIMIT = 40 * 1024 * 1024


def flipped(x, axis, mask):
    return lax.ppermute(x, axis, [(i, i ^ mask) for i in range(lax.axis_size(axis))])


def parity(bits, width):
    shift = 1 << (width - 1).bit_length() >> 1
    while shift:
        bits = bits ^ (bits >> shift)
        shift //= 2
    return bits & 1


def butterfly(parts):
    stride = 1
    while stride < len(parts):
        parts = [
            parts[i] + parts[i + stride] if not i & stride else parts[i - stride] - parts[i]
            for i in range(len(parts))
        ]
        stride *= 2
    return parts


def split(x):
    high = x.astype(jnp.bfloat16)
    return high, (x - high.astype(jnp.float32)).astype(jnp.bfloat16)


def dot(left, right):
    return jnp.dot(left, right, preferred_element_type=jnp.float32)


def prepare_kernel(acts_ref, signs_ref, index_ref, cots_ref, turned_ref, signs_out_ref, rows_ref, cots_out_ref):
    rows, breadth = signs_out_ref.shape
    spread = breadth // LANES
    for piece in range(spread):
        part = signs_ref[pl.ds(piece, rows, stride=spread), :]
        signs_out_ref[:, piece * LANES : (piece + 1) * LANES] = part.astype(jnp.float32).astype(jnp.bfloat16)
    turned_ref[...] = acts_ref[...].T
    cots_out_ref[...] = cots_ref[...]
    height = rows * pl.num_programs(0)
    index = index_ref[...]
    at_row = ((index >> LANE_BITS) & (spread - 1)) * height + ((index // breadth) & (height - 1))
    half = (index // (breadth * height)) & 1
    rows_ref[...] = half * (spread * height) + at_row


def sketch_kernel(parties, scale, own_turned, own_signs, other_acts, other_signs, index_ref, rows_hbm, *refs):
    outs = parties // 2
    chunk_refs, out_ref, scratch = refs[:parties], refs[parties], refs[parties + 1 :]
    table, cots, other_turned, total, change, result, rows_ref, rows_sems, *picked = scratch
    me = lax.axis_index("param")
    height, breadth = total.shape
    spread = breadth // LANES
    tokens = chunk_refs[0].shape[0]
    share = index_ref.shape[0] // parties

    def start_of(out):
        return pl.multiple_of((2 * out + (me & 1)) * share, share)

    copies = []
    for out in range(outs):
        source = rows_hbm.at[pl.ds(start_of(out), share), :]
        target = rows_ref.at[pl.ds(out * share, share), :]
        copies.append(pltpu.make_async_copy(source, target, rows_sems.at[out]))
    for copy in copies:
        copy.start()

    for distance in range(parties):
        start = pl.multiple_of((me ^ distance) * tokens, tokens)
        cots[pl.ds(start, tokens), :] = chunk_refs[distance][...]
    other_turned[...] = other_acts[...].T

    row_at = lax.broadcasted_iota(jnp.int32, (SIDE, SIDE), 0)
    col_at = lax.broadcasted_iota(jnp.int32, (SIDE, SIDE), 1)
    hadamard = (1 - 2 * parity(row_at & col_at, 8)).astype(jnp.float32).astype(jnp.bfloat16)

    row_blocks, col_blocks, pieces = height // SIDE, breadth // SIDE, SIDE // LANES
    for col in range(col_blocks):
        cols = slice(col * SIDE, (col + 1) * SIDE)
        own = dot(own_turned[...], cots[:, cols]) * own_signs[:, cols].astype(jnp.float32)
        strips = [other_signs[pl.ds(col * pieces + piece, height, stride=spread), :] for piece in range(pieces)]
        other = dot(other_turned[...], cots[:, cols]) * jnp.concatenate(strips, axis=1).astype(jnp.float32)
        for signed, product in ((total, own + other), (change, own - other)):
            parts = butterfly([product[row * SIDE : (row + 1) * SIDE] for row in range(row_blocks)])
            for row in range(row_blocks):
                signed[row * SIDE : (row + 1) * SIDE, cols] = parts[row]
    for half, signed in enumerate((total, change)):
        for row in range(row_blocks):
            rows = slice(row * SIDE, (row + 1) * SIDE)
            parts = butterfly([signed[rows, col * SIDE : (col + 1) * SIDE] for col in range(col_blocks)])
            for col in range(col_blocks):
                high, low = split(parts[col])
                high, low = split(dot(high, hadamard) + dot(low, hadamard))
                done = dot(hadamard, high) + dot(hadamard, low)
                for piece in range(pieces):
                    at = (half * spread + col * pieces + piece) * height + row * SIDE
                    table[at : at + SIDE, :] = done[:, piece * LANES : (piece + 1) * LANES]

    for copy in copies:
        copy.wait()
    groups = share * outs
    depth = len(picked)
    singles = table.reshape(table.shape[0], 1, LANES)
    sub_at = lax.broadcasted_iota(jnp.int32, (LANES, LANES), 0)

    def choose(group, rows):
        lane = index_ref[pl.ds(start_of(group // share) + group % share, 1), :] & (LANES - 1)
        chosen = jnp.where(sub_at == lane, rows[...].T, 0.0)
        result[pl.ds(group, 1), :] = jnp.sum(chosen, axis=0, keepdims=True)

    def step(at, carry):
        for slot in range(depth):
            group = at * depth + slot
            choose(jnp.maximum(group - 1, 0), picked[slot - 1])
            for first in range(0, LANES, SUBLANES):
                at_rows = [rows_ref[group, first + k] for k in range(SUBLANES)]
                lines = [jnp.broadcast_to(singles[row], (SUBLANES, LANES)) for row in at_rows]
                merged = lines[0]
                for k in range(1, SUBLANES):
                    merged = jnp.where(sub_at[:SUBLANES] == k, lines[k], merged)
                picked[slot][first : first + SUBLANES, :] = merged
        return carry

    lax.fori_loop(0, groups // depth, step, 0)
    choose(groups - 1, picked[-1])

    bits = (height * breadth).bit_length() - 1
    for out in range(outs):
        owner = index_ref[pl.ds(start_of(out), share), :] >> bits
        sign = (1 - 2 * parity(owner & me, parties.bit_length() - 1)).astype(jnp.float32)
        out_ref[out] = result[out * share : (out + 1) * share, :] * (sign * scale)


def on_device(activations, cotangents, signs, indices):
    tokens, height = activations.shape[1:]
    breadth = cotangents.shape[2]
    parties = lax.axis_size("param")
    samples = indices.shape[0]
    groups = samples // LANES
    table_rows = height * breadth // LANES
    outs = parties // 2
    vmem = pl.BlockSpec(memory_space=pltpu.VMEM)

    chunks = {0: cotangents[0]}
    for distance in range(2, parties, 2):
        chunks[distance] = flipped(chunks[0], "param", distance)
    acts = activations[0]
    sign_rows = signs.reshape(table_rows, LANES)
    index_rows = indices.reshape(groups, LANES)
    other_acts, other_signs = flipped(acts, "param", 1), flipped(sign_rows, "param", 1)

    steps = height // LANES
    turned, sign_matrix, rows, chunks[0] = pl.pallas_call(
        prepare_kernel,
        grid=(steps,),
        out_shape=[
            jax.ShapeDtypeStruct((height, tokens), jnp.bfloat16),
            jax.ShapeDtypeStruct((height, breadth), jnp.bfloat16),
            jax.ShapeDtypeStruct((groups, LANES), jnp.int32),
            jax.ShapeDtypeStruct(chunks[0].shape, jnp.bfloat16),
        ],
        in_specs=[
            pl.BlockSpec((tokens, LANES), lambda at: (0, at)),
            pl.BlockSpec((table_rows // steps, LANES), lambda at: (at, 0)),
            pl.BlockSpec((groups // steps, LANES), lambda at: (at, 0)),
            pl.BlockSpec((chunks[0].shape[0], breadth // steps), lambda at: (0, at)),
        ],
        out_specs=[
            pl.BlockSpec((LANES, tokens), lambda at: (at, 0)),
            pl.BlockSpec((LANES, breadth), lambda at: (at, 0)),
            pl.BlockSpec((groups // steps, LANES), lambda at: (at, 0)),
            pl.BlockSpec((chunks[0].shape[0], breadth // steps), lambda at: (0, at)),
        ],
        compiler_params=pltpu.CompilerParams(vmem_limit_bytes=LIMIT),
        cost_estimate=pl.CostEstimate(flops=0, bytes_accessed=8 * height * breadth, transcendentals=0),
        name="prepare",
    )(*[pltpu.with_memory_space_constraint(x, pltpu.HBM) for x in (acts, sign_rows, index_rows, chunks[0])])
    for distance in range(0, parties, 2):
        chunks[distance + 1] = flipped(chunks[distance], "param", 1)

    sums = pl.pallas_call(
        functools.partial(sketch_kernel, parties, 1.0 / math.sqrt(height * breadth * parties)),
        out_shape=jax.ShapeDtypeStruct((outs, groups // parties, LANES), jnp.float32),
        in_specs=[vmem] * 5 + [pl.BlockSpec(memory_space=pl.ANY)] + [vmem] * parties,
        out_specs=vmem,
        scratch_shapes=[
            pltpu.VMEM((2 * table_rows + SUBLANES, LANES), jnp.float32),
            pltpu.VMEM((tokens, breadth), jnp.bfloat16),
            pltpu.VMEM((height, tokens), jnp.bfloat16),
            pltpu.VMEM((height, breadth), jnp.float32),
            pltpu.VMEM((height, breadth), jnp.float32),
            pltpu.VMEM((groups // 2, LANES), jnp.float32),
            pltpu.SMEM((groups // 2, LANES), jnp.int32),
            pltpu.SemaphoreType.DMA((outs,)),
        ]
        + [pltpu.VMEM((LANES, LANES), jnp.float32)] * 4,
        compiler_params=pltpu.CompilerParams(vmem_limit_bytes=LIMIT),
        name="sketch",
    )(
        turned,
        sign_matrix,
        other_acts,
        other_signs,
        index_rows,
        rows,
        *[chunks[d] for d in range(parties)],
    )

    same_core = [list(range(core, parties, 2)) for core in range(2)]
    terms = lax.all_to_all(sums, "param", 0, 0, axis_index_groups=same_core)
    return jnp.sum(terms, axis=0).reshape(1, samples // parties)


def solution(mesh):
    in_specs = (P("ex", None, "param"), P("ex", "param", None), P("param"), P())
    out_specs = P("ex", "param")
    return jax.shard_map(
        on_device, mesh=mesh, in_specs=in_specs, out_specs=out_specs, check_vma=False
    )
```

```python
import functools
import math

import jax
import jax.numpy as jnp
from jax import lax
from jax.experimental import pallas as pl
from jax.experimental.pallas import tpu as pltpu
from jax.sharding import PartitionSpec as P

LANES = 128
LANE_BITS = 7
SIDE = 256
SUBLANES = 8
LIMIT = 40 * 1024 * 1024


def flipped(x, axis, mask):
    return lax.ppermute(x, axis, [(i, i ^ mask) for i in range(lax.axis_size(axis))])


def parity(bits, width):
    shift = 1 << (width - 1).bit_length() >> 1
    while shift:
        bits = bits ^ (bits >> shift)
        shift //= 2
    return bits & 1


def butterfly(parts):
    stride = 1
    while stride < len(parts):
        parts = [
            parts[i] + parts[i + stride] if not i & stride else parts[i - stride] - parts[i]
            for i in range(len(parts))
        ]
        stride *= 2
    return parts


def split(x):
    high = x.astype(jnp.bfloat16)
    return high, (x - high.astype(jnp.float32)).astype(jnp.bfloat16)


def dot(left, right):
    return jnp.dot(left, right, preferred_element_type=jnp.float32)


def prepare_kernel(acts_ref, signs_ref, index_ref, turned_ref, signs_out_ref, rows_ref):
    rows, breadth = signs_out_ref.shape
    spread = breadth // LANES
    for piece in range(spread):
        part = signs_ref[pl.ds(piece, rows, stride=spread), :]
        signs_out_ref[:, piece * LANES : (piece + 1) * LANES] = part.astype(jnp.float32).astype(jnp.bfloat16)
    turned_ref[...] = acts_ref[...].T
    height = rows * pl.num_programs(0)
    index = index_ref[...]
    at_row = ((index >> LANE_BITS) & (spread - 1)) * height + ((index // breadth) & (height - 1))
    half = (index // (breadth * height)) & 1
    rows_ref[...] = half * (spread * height) + at_row


def sketch_kernel(parties, scale, own_turned, own_signs, other_acts, other_signs, index_ref, rows_hbm, *refs):
    outs = parties // 2
    chunk_refs, out_refs, scratch = refs[:parties], refs[parties : parties + outs], refs[parties + outs :]
    table, cots, other_turned, total, change, result, rows_ref, rows_sems, *picked = scratch
    me = lax.axis_index("param")
    height, breadth = total.shape
    spread = breadth // LANES
    tokens = chunk_refs[0].shape[0]
    share = index_ref.shape[0] // parties

    def start_of(out):
        return pl.multiple_of((me ^ (2 * out)) * share, share)

    copies = []
    for out in range(outs):
        source = rows_hbm.at[pl.ds(start_of(out), share), :]
        target = rows_ref.at[pl.ds(out * share, share), :]
        copies.append(pltpu.make_async_copy(source, target, rows_sems.at[out]))
    for copy in copies:
        copy.start()

    for distance in range(parties):
        start = pl.multiple_of((me ^ distance) * tokens, tokens)
        cots[pl.ds(start, tokens), :] = chunk_refs[distance][...]
    other_turned[...] = other_acts[...].T

    row_at = lax.broadcasted_iota(jnp.int32, (SIDE, SIDE), 0)
    col_at = lax.broadcasted_iota(jnp.int32, (SIDE, SIDE), 1)
    hadamard = (1 - 2 * parity(row_at & col_at, 8)).astype(jnp.float32).astype(jnp.bfloat16)

    row_blocks, col_blocks, pieces = height // SIDE, breadth // SIDE, SIDE // LANES
    for col in range(col_blocks):
        cols = slice(col * SIDE, (col + 1) * SIDE)
        own = dot(own_turned[...], cots[:, cols]) * own_signs[:, cols].astype(jnp.float32)
        strips = [other_signs[pl.ds(col * pieces + piece, height, stride=spread), :] for piece in range(pieces)]
        other = dot(other_turned[...], cots[:, cols]) * jnp.concatenate(strips, axis=1).astype(jnp.float32)
        for signed, product in ((total, own + other), (change, own - other)):
            parts = butterfly([product[row * SIDE : (row + 1) * SIDE] for row in range(row_blocks)])
            for row in range(row_blocks):
                signed[row * SIDE : (row + 1) * SIDE, cols] = parts[row]
    for half, signed in enumerate((total, change)):
        for row in range(row_blocks):
            rows = slice(row * SIDE, (row + 1) * SIDE)
            parts = butterfly([signed[rows, col * SIDE : (col + 1) * SIDE] for col in range(col_blocks)])
            for col in range(col_blocks):
                high, low = split(parts[col])
                high, low = split(dot(high, hadamard) + dot(low, hadamard))
                done = dot(hadamard, high) + dot(hadamard, low)
                for piece in range(pieces):
                    at = (half * spread + col * pieces + piece) * height + row * SIDE
                    table[at : at + SIDE, :] = done[:, piece * LANES : (piece + 1) * LANES]

    for copy in copies:
        copy.wait()
    groups = share * outs
    depth = len(picked)
    singles = table.reshape(table.shape[0], 1, LANES)
    sub_at = lax.broadcasted_iota(jnp.int32, (LANES, LANES), 0)

    def choose(group, rows):
        lane = index_ref[pl.ds(start_of(group // share) + group % share, 1), :] & (LANES - 1)
        chosen = jnp.where(sub_at == lane, rows[...].T, 0.0)
        result[pl.ds(group, 1), :] = jnp.sum(chosen, axis=0, keepdims=True)

    def step(at, carry):
        for slot in range(depth):
            group = at * depth + slot
            choose(jnp.maximum(group - 1, 0), picked[slot - 1])
            for first in range(0, LANES, SUBLANES):
                at_rows = [rows_ref[group, first + k] for k in range(SUBLANES)]
                lines = [jnp.broadcast_to(singles[row], (SUBLANES, LANES)) for row in at_rows]
                merged = lines[0]
                for k in range(1, SUBLANES):
                    merged = jnp.where(sub_at[:SUBLANES] == k, lines[k], merged)
                picked[slot][first : first + SUBLANES, :] = merged
        return carry

    lax.fori_loop(0, groups // depth, step, 0)
    choose(groups - 1, picked[-1])

    bits = (height * breadth).bit_length() - 1
    for out, out_ref in enumerate(out_refs):
        owner = index_ref[pl.ds(start_of(out), share), :] >> bits
        sign = (1 - 2 * parity(owner & me, parties.bit_length() - 1)).astype(jnp.float32)
        out_ref[...] = result[out * share : (out + 1) * share, :] * (sign * scale)


def on_device(activations, cotangents, signs, indices):
    tokens, height = activations.shape[1:]
    breadth = cotangents.shape[2]
    parties = lax.axis_size("param")
    samples = indices.shape[0]
    groups = samples // LANES
    table_rows = height * breadth // LANES
    outs = parties // 2
    vmem = pl.BlockSpec(memory_space=pltpu.VMEM)

    chunks = {0: cotangents[0]}
    for distance in range(2, parties, 2):
        chunks[distance] = flipped(chunks[0], "param", distance)
    acts = activations[0]
    sign_rows = signs.reshape(table_rows, LANES)
    index_rows = indices.reshape(groups, LANES)
    other_acts, other_signs = flipped(acts, "param", 1), flipped(sign_rows, "param", 1)

    steps = height // LANES
    turned, sign_matrix, rows = pl.pallas_call(
        prepare_kernel,
        grid=(steps,),
        out_shape=[
            jax.ShapeDtypeStruct((height, tokens), jnp.bfloat16),
            jax.ShapeDtypeStruct((height, breadth), jnp.bfloat16),
            jax.ShapeDtypeStruct((groups, LANES), jnp.int32),
        ],
        in_specs=[
            pl.BlockSpec((tokens, LANES), lambda at: (0, at)),
            pl.BlockSpec((table_rows // steps, LANES), lambda at: (at, 0)),
            pl.BlockSpec((groups // steps, LANES), lambda at: (at, 0)),
        ],
        out_specs=[
            pl.BlockSpec((LANES, tokens), lambda at: (at, 0)),
            pl.BlockSpec((LANES, breadth), lambda at: (at, 0)),
            pl.BlockSpec((groups // steps, LANES), lambda at: (at, 0)),
        ],
        compiler_params=pltpu.CompilerParams(vmem_limit_bytes=LIMIT),
        cost_estimate=pl.CostEstimate(flops=0, bytes_accessed=8 * height * breadth, transcendentals=0),
        name="prepare",
    )(*[pltpu.with_memory_space_constraint(x, pltpu.HBM) for x in (acts, sign_rows, index_rows)])
    chunks[0], rows = lax.optimization_barrier((chunks[0], rows))
    for distance in range(0, parties, 2):
        chunks[distance + 1] = flipped(chunks[distance], "param", 1)

    sums = pl.pallas_call(
        functools.partial(sketch_kernel, parties, 1.0 / math.sqrt(height * breadth * parties)),
        out_shape=[jax.ShapeDtypeStruct((groups // parties, LANES), jnp.float32)] * outs,
        in_specs=[vmem] * 5 + [pl.BlockSpec(memory_space=pl.ANY)] + [vmem] * parties,
        out_specs=[vmem] * outs,
        scratch_shapes=[
            pltpu.VMEM((2 * table_rows + SUBLANES, LANES), jnp.float32),
            pltpu.VMEM((tokens, breadth), jnp.bfloat16),
            pltpu.VMEM((height, tokens), jnp.bfloat16),
            pltpu.VMEM((height, breadth), jnp.float32),
            pltpu.VMEM((height, breadth), jnp.float32),
            pltpu.VMEM((groups // 2, LANES), jnp.float32),
            pltpu.SMEM((groups // 2, LANES), jnp.int32),
            pltpu.SemaphoreType.DMA((outs,)),
        ]
        + [pltpu.VMEM((LANES, LANES), jnp.float32)] * 8,
        compiler_params=pltpu.CompilerParams(vmem_limit_bytes=LIMIT),
        name="sketch",
    )(
        turned,
        sign_matrix,
        other_acts,
        other_signs,
        index_rows,
        rows,
        *[chunks[d] for d in range(parties)],
    )

    total = sums[0]
    for out in range(1, outs):
        total = total + flipped(sums[out], "param", 2 * out)
    return total.reshape(1, samples // parties)


def solution(mesh):
    in_specs = (P("ex", None, "param"), P("ex", "param", None), P("param"), P())
    out_specs = P("ex", "param")
    return jax.shard_map(
        on_device, mesh=mesh, in_specs=in_specs, out_specs=out_specs, check_vma=False
    )
```

```python
import functools
import math

import jax
import jax.numpy as jnp
from jax import lax
from jax.experimental import pallas as pl
from jax.experimental.pallas import tpu as pltpu
from jax.sharding import PartitionSpec as P

LANES = 128
LANE_BITS = 7
HALF_WORD = 16
SIDE = 256
SUBLANES = 8
LIMIT = 40 * 1024 * 1024


def flipped(x, axis, mask):
    return lax.ppermute(x, axis, [(i, i ^ mask) for i in range(lax.axis_size(axis))])


def parity(bits, width):
    shift = 1 << (width - 1).bit_length() >> 1
    while shift:
        bits = bits ^ (bits >> shift)
        shift //= 2
    return bits & 1


def butterfly(parts):
    stride = 1
    while stride < len(parts):
        parts = [
            parts[i] + parts[i + stride] if not i & stride else parts[i - stride] - parts[i]
            for i in range(len(parts))
        ]
        stride *= 2
    return parts


def split(x):
    high = x.astype(jnp.bfloat16)
    return high, (x - high.astype(jnp.float32)).astype(jnp.bfloat16)


def dot(left, right):
    return jnp.dot(left, right, preferred_element_type=jnp.float32)


def prepare_kernel(acts_ref, signs_ref, index_ref, turned_ref, signs_out_ref, rows_ref):
    rows, breadth = signs_out_ref.shape
    spread = breadth // LANES
    for piece in range(spread):
        part = signs_ref[pl.ds(piece, rows, stride=spread), :]
        signs_out_ref[:, piece * LANES : (piece + 1) * LANES] = part.astype(jnp.float32).astype(jnp.bfloat16)
    turned_ref[...] = acts_ref[...].T
    height = rows * pl.num_programs(0)
    index = index_ref[...]
    at_row = ((index >> LANE_BITS) & (spread - 1)) * height + ((index // breadth) & (height - 1))
    half = (index // (breadth * height)) & 1
    at_row = half * (spread * height) + at_row
    rows_ref[...] = at_row | (pltpu.roll(at_row, LANES // 2, 1) << HALF_WORD)


def sketch_kernel(parties, scale, own_turned, own_signs, other_acts, other_signs, index_ref, rows_hbm, *refs):
    outs = parties // 2
    chunk_refs, out_refs, scratch = refs[:parties], refs[parties : parties + outs], refs[parties + outs :]
    table, cots, other_turned, total, change, result, rows_ref, rows_sems, *picked = scratch
    me = lax.axis_index("param")
    height, breadth = total.shape
    spread = breadth // LANES
    tokens = chunk_refs[0].shape[0]
    share = index_ref.shape[0] // parties

    def start_of(out):
        return pl.multiple_of((me ^ (2 * out)) * share, share)

    copies = []
    for out in range(outs):
        source = rows_hbm.at[pl.ds(start_of(out), share), :]
        target = rows_ref.at[pl.ds(out * share, share), :]
        copies.append(pltpu.make_async_copy(source, target, rows_sems.at[out]))
    for copy in copies:
        copy.start()

    for distance in range(parties):
        start = pl.multiple_of((me ^ distance) * tokens, tokens)
        cots[pl.ds(start, tokens), :] = chunk_refs[distance][...]
    other_turned[...] = other_acts[...].T

    row_at = lax.broadcasted_iota(jnp.int32, (SIDE, SIDE), 0)
    col_at = lax.broadcasted_iota(jnp.int32, (SIDE, SIDE), 1)
    hadamard = (1 - 2 * parity(row_at & col_at, 8)).astype(jnp.float32).astype(jnp.bfloat16)

    row_blocks, col_blocks, pieces = height // SIDE, breadth // SIDE, SIDE // LANES
    for col in range(col_blocks):
        cols = slice(col * SIDE, (col + 1) * SIDE)
        own = dot(own_turned[...], cots[:, cols]) * own_signs[:, cols].astype(jnp.float32)
        strips = [other_signs[pl.ds(col * pieces + piece, height, stride=spread), :] for piece in range(pieces)]
        other = dot(other_turned[...], cots[:, cols]) * jnp.concatenate(strips, axis=1).astype(jnp.float32)
        for signed, product in ((total, own + other), (change, own - other)):
            parts = butterfly([product[row * SIDE : (row + 1) * SIDE] for row in range(row_blocks)])
            for row in range(row_blocks):
                signed[row * SIDE : (row + 1) * SIDE, cols] = parts[row]
    for half, signed in enumerate((total, change)):
        for row in range(row_blocks):
            rows = slice(row * SIDE, (row + 1) * SIDE)
            parts = butterfly([signed[rows, col * SIDE : (col + 1) * SIDE] for col in range(col_blocks)])
            for col in range(col_blocks):
                high, low = split(parts[col])
                high, low = split(dot(high, hadamard) + dot(low, hadamard))
                done = dot(hadamard, high) + dot(hadamard, low)
                for piece in range(pieces):
                    at = (half * spread + col * pieces + piece) * height + row * SIDE
                    table[at : at + SIDE, :] = done[:, piece * LANES : (piece + 1) * LANES]

    for copy in copies:
        copy.wait()
    groups = share * outs
    depth = len(picked)
    singles = table.reshape(table.shape[0], 1, LANES)
    sub_at = lax.broadcasted_iota(jnp.int32, (LANES, LANES), 0)

    def choose(group, rows):
        lane = index_ref[pl.ds(start_of(group // share) + group % share, 1), :] & (LANES - 1)
        chosen = jnp.where(sub_at == lane, rows[...].T, 0.0)
        result[pl.ds(group, 1), :] = jnp.sum(chosen, axis=0, keepdims=True)

    def step(at, carry):
        for slot in range(depth):
            group = at * depth + slot
            choose(jnp.maximum(group - 1, 0), picked[slot - 1])
            for first in range(0, LANES // 2, SUBLANES):
                words = [rows_ref[group, first + k] for k in range(SUBLANES)]
                low = [word & ((1 << HALF_WORD) - 1) for word in words]
                high = [word >> HALF_WORD for word in words]
                for at_rows, to in ((low, first), (high, first + LANES // 2)):
                    lines = [jnp.broadcast_to(singles[row], (SUBLANES, LANES)) for row in at_rows]
                    merged = lines[0]
                    for k in range(1, SUBLANES):
                        merged = jnp.where(sub_at[:SUBLANES] == k, lines[k], merged)
                    picked[slot][to : to + SUBLANES, :] = merged
        return carry

    lax.fori_loop(0, groups // depth, step, 0)
    choose(groups - 1, picked[-1])

    bits = (height * breadth).bit_length() - 1
    for out, out_ref in enumerate(out_refs):
        owner = index_ref[pl.ds(start_of(out), share), :] >> bits
        sign = (1 - 2 * parity(owner & me, parties.bit_length() - 1)).astype(jnp.float32)
        out_ref[...] = result[out * share : (out + 1) * share, :] * (sign * scale)


def on_device(activations, cotangents, signs, indices):
    tokens, height = activations.shape[1:]
    breadth = cotangents.shape[2]
    parties = lax.axis_size("param")
    samples = indices.shape[0]
    groups = samples // LANES
    table_rows = height * breadth // LANES
    outs = parties // 2
    vmem = pl.BlockSpec(memory_space=pltpu.VMEM)

    chunks = {0: cotangents[0]}
    for distance in range(2, parties, 2):
        chunks[distance] = flipped(chunks[0], "param", distance)
    acts = activations[0]
    sign_rows = signs.reshape(table_rows, LANES)
    index_rows = indices.reshape(groups, LANES)
    other_acts, other_signs = flipped(acts, "param", 1), flipped(sign_rows, "param", 1)

    steps = height // LANES
    turned, sign_matrix, rows = pl.pallas_call(
        prepare_kernel,
        grid=(steps,),
        out_shape=[
            jax.ShapeDtypeStruct((height, tokens), jnp.bfloat16),
            jax.ShapeDtypeStruct((height, breadth), jnp.bfloat16),
            jax.ShapeDtypeStruct((groups, LANES), jnp.int32),
        ],
        in_specs=[
            pl.BlockSpec((tokens, LANES), lambda at: (0, at)),
            pl.BlockSpec((table_rows // steps, LANES), lambda at: (at, 0)),
            pl.BlockSpec((groups // steps, LANES), lambda at: (at, 0)),
        ],
        out_specs=[
            pl.BlockSpec((LANES, tokens), lambda at: (at, 0)),
            pl.BlockSpec((LANES, breadth), lambda at: (at, 0)),
            pl.BlockSpec((groups // steps, LANES), lambda at: (at, 0)),
        ],
        compiler_params=pltpu.CompilerParams(vmem_limit_bytes=LIMIT),
        cost_estimate=pl.CostEstimate(flops=0, bytes_accessed=8 * height * breadth, transcendentals=0),
        name="prepare",
    )(*[pltpu.with_memory_space_constraint(x, pltpu.HBM) for x in (acts, sign_rows, index_rows)])
    chunks[0], rows = lax.optimization_barrier((chunks[0], rows))
    for distance in range(0, parties, 2):
        chunks[distance + 1] = flipped(chunks[distance], "param", 1)

    sums = pl.pallas_call(
        functools.partial(sketch_kernel, parties, 1.0 / math.sqrt(height * breadth * parties)),
        out_shape=[jax.ShapeDtypeStruct((groups // parties, LANES), jnp.float32)] * outs,
        in_specs=[vmem] * 5 + [pl.BlockSpec(memory_space=pl.ANY)] + [vmem] * parties,
        out_specs=[vmem] * outs,
        scratch_shapes=[
            pltpu.VMEM((2 * table_rows + SUBLANES, LANES), jnp.float32),
            pltpu.VMEM((tokens, breadth), jnp.bfloat16),
            pltpu.VMEM((height, tokens), jnp.bfloat16),
            pltpu.VMEM((height, breadth), jnp.float32),
            pltpu.VMEM((height, breadth), jnp.float32),
            pltpu.VMEM((groups // 2, LANES), jnp.float32),
            pltpu.SMEM((groups // 2, LANES), jnp.int32),
            pltpu.SemaphoreType.DMA((outs,)),
        ]
        + [pltpu.VMEM((LANES, LANES), jnp.float32)] * 8,
        compiler_params=pltpu.CompilerParams(vmem_limit_bytes=LIMIT),
        name="sketch",
    )(
        turned,
        sign_matrix,
        other_acts,
        other_signs,
        index_rows,
        rows,
        *[chunks[d] for d in range(parties)],
    )

    total = sums[0]
    for out in range(1, outs):
        total = total + flipped(sums[out], "param", 2 * out)
    return total.reshape(1, samples // parties)


def solution(mesh):
    in_specs = (P("ex", None, "param"), P("ex", "param", None), P("param"), P())
    out_specs = P("ex", "param")
    return jax.shard_map(
        on_device, mesh=mesh, in_specs=in_specs, out_specs=out_specs, check_vma=False
    )
```

```python
import functools
import math

import jax
import jax.numpy as jnp
from jax import lax
from jax.experimental import pallas as pl
from jax.experimental.pallas import tpu as pltpu
from jax.sharding import PartitionSpec as P

LANES = 128
LANE_BITS = 7
SIDE = 256
SUBLANES = 8
DEPTH = 8
LIMIT = 40 * 1024 * 1024


def flipped(x, axis, mask):
    return lax.ppermute(x, axis, [(i, i ^ mask) for i in range(lax.axis_size(axis))])


def parity(bits, width):
    shift = 1 << (width - 1).bit_length() >> 1
    while shift:
        bits = bits ^ (bits >> shift)
        shift //= 2
    return bits & 1


def butterfly(parts):
    stride = 1
    while stride < len(parts):
        parts = [
            parts[i] + parts[i + stride] if not i & stride else parts[i - stride] - parts[i]
            for i in range(len(parts))
        ]
        stride *= 2
    return parts


def split(x):
    high = x.astype(jnp.bfloat16)
    return high, (x - high.astype(jnp.float32)).astype(jnp.bfloat16)


def dot(left, right):
    return jnp.dot(left, right, preferred_element_type=jnp.float32)


def prepare_kernel(acts_ref, signs_ref, index_ref, turned_ref, signs_out_ref, rows_ref):
    rows, breadth = signs_out_ref.shape
    spread = breadth // LANES
    for piece in range(spread):
        part = signs_ref[pl.ds(piece, rows, stride=spread), :]
        signs_out_ref[:, piece * LANES : (piece + 1) * LANES] = part.astype(jnp.float32).astype(jnp.bfloat16)
    turned_ref[...] = acts_ref[...].T
    height = rows * pl.num_programs(0)
    index = index_ref[...]
    at_row = ((index >> LANE_BITS) & (spread - 1)) * height + ((index // breadth) & (height - 1))
    half = (index // (breadth * height)) & 1
    rows_ref[...] = half * (spread * height) + at_row


def sketch_kernel(parties, scale, own_turned, own_signs, other_acts, other_signs, index_ref, rows_hbm, *refs):
    outs = parties // 2
    chunk_refs, out_refs, scratch = refs[:parties], refs[parties : parties + outs], refs[parties + outs :]
    table, cots, other_turned, total, change, result, rows_even, rows_odd, rows_sems, *picked = scratch
    me = lax.axis_index("param")
    height, breadth = total.shape
    spread = breadth // LANES
    tokens = chunk_refs[0].shape[0]
    share = index_ref.shape[0] // parties

    def start_of(out):
        return pl.multiple_of((me ^ (2 * out)) * share, share)

    groups = share * outs
    depth = len(picked)
    last = groups // depth - 1

    def fetch(batch):
        group = jnp.minimum(batch, last) * depth
        start = pl.multiple_of(start_of(group // share) + group % share, depth)
        return pl.ds(start, depth)

    def fetched(batch, parity_at):
        target = (rows_even, rows_odd)[parity_at]
        return pltpu.make_async_copy(rows_hbm.at[fetch(batch), :], target, rows_sems.at[parity_at])

    fetched(0, 0).start()
    fetched(1, 1).start()

    for distance in range(parties):
        start = pl.multiple_of((me ^ distance) * tokens, tokens)
        cots[pl.ds(start, tokens), :] = chunk_refs[distance][...]
    other_turned[...] = other_acts[...].T

    row_at = lax.broadcasted_iota(jnp.int32, (SIDE, SIDE), 0)
    col_at = lax.broadcasted_iota(jnp.int32, (SIDE, SIDE), 1)
    hadamard = (1 - 2 * parity(row_at & col_at, 8)).astype(jnp.float32).astype(jnp.bfloat16)

    row_blocks, col_blocks, pieces = height // SIDE, breadth // SIDE, SIDE // LANES
    for col in range(col_blocks):
        cols = slice(col * SIDE, (col + 1) * SIDE)
        own = dot(own_turned[...], cots[:, cols]) * own_signs[:, cols].astype(jnp.float32)
        strips = [other_signs[pl.ds(col * pieces + piece, height, stride=spread), :] for piece in range(pieces)]
        other = dot(other_turned[...], cots[:, cols]) * jnp.concatenate(strips, axis=1).astype(jnp.float32)
        for signed, product in ((total, own + other), (change, own - other)):
            parts = butterfly([product[row * SIDE : (row + 1) * SIDE] for row in range(row_blocks)])
            for row in range(row_blocks):
                signed[row * SIDE : (row + 1) * SIDE, cols] = parts[row]
    for half, signed in enumerate((total, change)):
        for row in range(row_blocks):
            rows = slice(row * SIDE, (row + 1) * SIDE)
            parts = butterfly([signed[rows, col * SIDE : (col + 1) * SIDE] for col in range(col_blocks)])
            for col in range(col_blocks):
                high, low = split(parts[col])
                high, low = split(dot(high, hadamard) + dot(low, hadamard))
                done = dot(hadamard, high) + dot(hadamard, low)
                for piece in range(pieces):
                    at = (half * spread + col * pieces + piece) * height + row * SIDE
                    table[at : at + SIDE, :] = done[:, piece * LANES : (piece + 1) * LANES]

    singles = table.reshape(table.shape[0], 1, LANES)
    sub_at = lax.broadcasted_iota(jnp.int32, (LANES, LANES), 0)

    def choose(group, rows):
        lane = index_ref[pl.ds(start_of(group // share) + group % share, 1), :] & (LANES - 1)
        chosen = jnp.where(sub_at == lane, rows[...].T, 0.0)
        result[pl.ds(group, 1), :] = jnp.sum(chosen, axis=0, keepdims=True)

    def step(at, carry):
        for half, rows_ref in enumerate((rows_even, rows_odd)):
            batch = 2 * at + half
            fetched(batch, half).wait()
            for slot in range(depth):
                group = batch * depth + slot
                choose(jnp.maximum(group - 1, 0), picked[slot - 1])
                for first in range(0, LANES, SUBLANES):
                    at_rows = [rows_ref[slot, first + k] for k in range(SUBLANES)]
                    lines = [jnp.broadcast_to(singles[row], (SUBLANES, LANES)) for row in at_rows]
                    merged = lines[0]
                    for k in range(1, SUBLANES):
                        merged = jnp.where(sub_at[:SUBLANES] == k, lines[k], merged)
                    picked[slot][first : first + SUBLANES, :] = merged
            fetched(batch + 2, half).start()
        return carry

    lax.fori_loop(0, groups // depth // 2, step, 0)
    for half in range(2):
        fetched(last, half).wait()
    choose(groups - 1, picked[-1])

    bits = (height * breadth).bit_length() - 1
    for out, out_ref in enumerate(out_refs):
        owner = index_ref[pl.ds(start_of(out), share), :] >> bits
        sign = (1 - 2 * parity(owner & me, parties.bit_length() - 1)).astype(jnp.float32)
        out_ref[...] = result[out * share : (out + 1) * share, :] * (sign * scale)


def on_device(activations, cotangents, signs, indices):
    tokens, height = activations.shape[1:]
    breadth = cotangents.shape[2]
    parties = lax.axis_size("param")
    samples = indices.shape[0]
    groups = samples // LANES
    table_rows = height * breadth // LANES
    outs = parties // 2
    vmem = pl.BlockSpec(memory_space=pltpu.VMEM)

    chunks = {0: cotangents[0]}
    for distance in range(2, parties, 2):
        chunks[distance] = flipped(chunks[0], "param", distance)
    acts = activations[0]
    sign_rows = signs.reshape(table_rows, LANES)
    index_rows = indices.reshape(groups, LANES)
    other_acts, other_signs = flipped(acts, "param", 1), flipped(sign_rows, "param", 1)

    steps = height // LANES
    turned, sign_matrix, rows = pl.pallas_call(
        prepare_kernel,
        grid=(steps,),
        out_shape=[
            jax.ShapeDtypeStruct((height, tokens), jnp.bfloat16),
            jax.ShapeDtypeStruct((height, breadth), jnp.bfloat16),
            jax.ShapeDtypeStruct((groups, LANES), jnp.int32),
        ],
        in_specs=[
            pl.BlockSpec((tokens, LANES), lambda at: (0, at)),
            pl.BlockSpec((table_rows // steps, LANES), lambda at: (at, 0)),
            pl.BlockSpec((groups // steps, LANES), lambda at: (at, 0)),
        ],
        out_specs=[
            pl.BlockSpec((LANES, tokens), lambda at: (at, 0)),
            pl.BlockSpec((LANES, breadth), lambda at: (at, 0)),
            pl.BlockSpec((groups // steps, LANES), lambda at: (at, 0)),
        ],
        compiler_params=pltpu.CompilerParams(vmem_limit_bytes=LIMIT),
        cost_estimate=pl.CostEstimate(flops=0, bytes_accessed=8 * height * breadth, transcendentals=0),
        name="prepare",
    )(*[pltpu.with_memory_space_constraint(x, pltpu.HBM) for x in (acts, sign_rows, index_rows)])
    chunks[0], rows = lax.optimization_barrier((chunks[0], rows))
    for distance in range(0, parties, 2):
        chunks[distance + 1] = flipped(chunks[distance], "param", 1)

    sums = pl.pallas_call(
        functools.partial(sketch_kernel, parties, 1.0 / math.sqrt(height * breadth * parties)),
        out_shape=[jax.ShapeDtypeStruct((groups // parties, LANES), jnp.float32)] * outs,
        in_specs=[vmem] * 5 + [pl.BlockSpec(memory_space=pl.ANY)] + [vmem] * parties,
        out_specs=[vmem] * outs,
        scratch_shapes=[
            pltpu.VMEM((2 * table_rows + SUBLANES, LANES), jnp.float32),
            pltpu.VMEM((tokens, breadth), jnp.bfloat16),
            pltpu.VMEM((height, tokens), jnp.bfloat16),
            pltpu.VMEM((height, breadth), jnp.float32),
            pltpu.VMEM((height, breadth), jnp.float32),
            pltpu.VMEM((groups // 2, LANES), jnp.float32),
            pltpu.SMEM((DEPTH, LANES), jnp.int32),
            pltpu.SMEM((DEPTH, LANES), jnp.int32),
            pltpu.SemaphoreType.DMA((2,)),
        ]
        + [pltpu.VMEM((LANES, LANES), jnp.float32)] * DEPTH,
        compiler_params=pltpu.CompilerParams(vmem_limit_bytes=LIMIT),
        name="sketch",
    )(
        turned,
        sign_matrix,
        other_acts,
        other_signs,
        index_rows,
        rows,
        *[chunks[d] for d in range(parties)],
    )

    total = sums[0]
    for out in range(1, outs):
        total = total + flipped(sums[out], "param", 2 * out)
    return total.reshape(1, samples // parties)


def solution(mesh):
    in_specs = (P("ex", None, "param"), P("ex", "param", None), P("param"), P())
    out_specs = P("ex", "param")
    return jax.shard_map(
        on_device, mesh=mesh, in_specs=in_specs, out_specs=out_specs, check_vma=False
    )
```

```python
import functools
import math

import jax
import jax.numpy as jnp
from jax import lax
from jax.experimental import pallas as pl
from jax.experimental.pallas import tpu as pltpu
from jax.sharding import PartitionSpec as P

LANES = 128
LANE_BITS = 7
SIDE = 256
SUBLANES = 8
DEPTH = 16
LIMIT = 40 * 1024 * 1024


def flipped(x, axis, mask):
    return lax.ppermute(x, axis, [(i, i ^ mask) for i in range(lax.axis_size(axis))])


def parity(bits, width):
    shift = 1 << (width - 1).bit_length() >> 1
    while shift:
        bits = bits ^ (bits >> shift)
        shift //= 2
    return bits & 1


def butterfly(parts):
    stride = 1
    while stride < len(parts):
        parts = [
            parts[i] + parts[i + stride] if not i & stride else parts[i - stride] - parts[i]
            for i in range(len(parts))
        ]
        stride *= 2
    return parts


def split(x):
    high = x.astype(jnp.bfloat16)
    return high, (x - high.astype(jnp.float32)).astype(jnp.bfloat16)


def dot(left, right):
    return jnp.dot(left, right, preferred_element_type=jnp.float32)


def prepare_kernel(acts_ref, signs_ref, index_ref, turned_ref, signs_out_ref, rows_ref):
    rows, breadth = signs_out_ref.shape
    spread = breadth // LANES
    for piece in range(spread):
        part = signs_ref[pl.ds(piece, rows, stride=spread), :]
        signs_out_ref[:, piece * LANES : (piece + 1) * LANES] = part.astype(jnp.float32).astype(jnp.bfloat16)
    turned_ref[...] = acts_ref[...].T
    height = rows * pl.num_programs(0)
    index = index_ref[...]
    at_row = ((index >> LANE_BITS) & (spread - 1)) * height + ((index // breadth) & (height - 1))
    half = (index // (breadth * height)) & 1
    rows_ref[...] = half * (spread * height) + at_row


def sketch_kernel(parties, scale, own_turned, own_signs, other_acts, other_signs, index_ref, rows_hbm, *refs):
    outs = parties // 2
    chunk_refs, out_refs, scratch = refs[:parties], refs[parties : parties + outs], refs[parties + outs :]
    table, cots, other_turned, total, change, result, rows_even, rows_odd, rows_sems, *picked = scratch
    me = lax.axis_index("param")
    height, breadth = total.shape
    spread = breadth // LANES
    tokens = chunk_refs[0].shape[0]
    share = index_ref.shape[0] // parties

    def start_of(out):
        return pl.multiple_of((me ^ (2 * out)) * share, share)

    groups = share * outs
    depth = len(picked)
    last = groups // depth - 1

    def fetch(batch):
        group = jnp.minimum(batch, last) * depth
        start = pl.multiple_of(start_of(group // share) + group % share, depth)
        return pl.ds(start, depth)

    def fetched(batch, parity_at):
        target = (rows_even, rows_odd)[parity_at]
        return pltpu.make_async_copy(rows_hbm.at[fetch(batch), :], target, rows_sems.at[parity_at])

    fetched(0, 0).start()
    fetched(1, 1).start()

    for distance in range(parties):
        start = pl.multiple_of((me ^ distance) * tokens, tokens)
        cots[pl.ds(start, tokens), :] = chunk_refs[distance][...]

    row_at = lax.broadcasted_iota(jnp.int32, (SIDE, SIDE), 0)
    col_at = lax.broadcasted_iota(jnp.int32, (SIDE, SIDE), 1)
    hadamard = (1 - 2 * parity(row_at & col_at, 8)).astype(jnp.float32).astype(jnp.bfloat16)

    tall = jnp.concatenate([hadamard, hadamard], axis=0)
    wide = jnp.concatenate([hadamard, hadamard], axis=1)

    row_blocks, col_blocks, pieces = height // SIDE, breadth // SIDE, SIDE // LANES
    for col in range(col_blocks):
        cols = slice(col * SIDE, (col + 1) * SIDE)
        own = dot(own_turned[...], cots[:, cols]) * own_signs[:, cols].astype(jnp.float32)
        if col == 0:
            other_turned[...] = other_acts[...].T
        strips = [other_signs[pl.ds(col * pieces + piece, height, stride=spread), :] for piece in range(pieces)]
        other = dot(other_turned[...], cots[:, cols]) * jnp.concatenate(strips, axis=1).astype(jnp.float32)
        for signed, product in ((total, own + other), (change, own - other)):
            parts = butterfly([product[row * SIDE : (row + 1) * SIDE] for row in range(row_blocks)])
            for row in range(row_blocks):
                signed[row * SIDE : (row + 1) * SIDE, cols] = parts[row]
    for half, signed in enumerate((total, change)):
        for row in range(row_blocks):
            rows = slice(row * SIDE, (row + 1) * SIDE)
            parts = butterfly([signed[rows, col * SIDE : (col + 1) * SIDE] for col in range(col_blocks)])
            for col in range(col_blocks):
                half_done = dot(jnp.concatenate(split(parts[col]), axis=1), tall)
                done = dot(wide, jnp.concatenate(split(half_done), axis=0))
                for piece in range(pieces):
                    at = (half * spread + col * pieces + piece) * height + row * SIDE
                    table[at : at + SIDE, :] = done[:, piece * LANES : (piece + 1) * LANES]

    singles = table.reshape(table.shape[0], 1, LANES)
    sub_at = lax.broadcasted_iota(jnp.int32, (LANES, LANES), 0)

    def choose(group, rows):
        lane = index_ref[pl.ds(start_of(group // share) + group % share, 1), :] & (LANES - 1)
        chosen = jnp.where(sub_at == lane, rows[...].T, 0.0)
        result[pl.ds(group, 1), :] = jnp.sum(chosen, axis=0, keepdims=True)

    def step(at, carry):
        for half, rows_ref in enumerate((rows_even, rows_odd)):
            batch = 2 * at + half
            fetched(batch, half).wait()
            for slot in range(depth):
                group = batch * depth + slot
                choose(jnp.maximum(group - 1, 0), picked[slot - 1])
                for first in range(0, LANES, SUBLANES):
                    at_rows = [rows_ref[slot, first + k] for k in range(SUBLANES)]
                    lines = [jnp.broadcast_to(singles[row], (SUBLANES, LANES)) for row in at_rows]
                    merged = lines[0]
                    for k in range(1, SUBLANES):
                        merged = jnp.where(sub_at[:SUBLANES] == k, lines[k], merged)
                    picked[slot][first : first + SUBLANES, :] = merged
            fetched(batch + 2, half).start()
        return carry

    lax.fori_loop(0, groups // depth // 2, step, 0)
    for half in range(2):
        fetched(last, half).wait()
    choose(groups - 1, picked[-1])

    bits = (height * breadth).bit_length() - 1
    for out, out_ref in enumerate(out_refs):
        owner = index_ref[pl.ds(start_of(out), share), :] >> bits
        sign = (1 - 2 * parity(owner & me, parties.bit_length() - 1)).astype(jnp.float32)
        out_ref[...] = result[out * share : (out + 1) * share, :] * (sign * scale)


def on_device(activations, cotangents, signs, indices):
    tokens, height = activations.shape[1:]
    breadth = cotangents.shape[2]
    parties = lax.axis_size("param")
    samples = indices.shape[0]
    groups = samples // LANES
    table_rows = height * breadth // LANES
    outs = parties // 2
    depth = min(DEPTH, groups // parties)
    vmem = pl.BlockSpec(memory_space=pltpu.VMEM)

    chunks = {0: cotangents[0]}
    for distance in range(2, parties, 2):
        chunks[distance] = flipped(chunks[0], "param", distance)
    acts = activations[0]
    sign_rows = signs.reshape(table_rows, LANES)
    index_rows = indices.reshape(groups, LANES)
    other_acts, other_signs = flipped(acts, "param", 1), flipped(sign_rows, "param", 1)

    steps = height // LANES
    turned, sign_matrix, rows = pl.pallas_call(
        prepare_kernel,
        grid=(steps,),
        out_shape=[
            jax.ShapeDtypeStruct((height, tokens), jnp.bfloat16),
            jax.ShapeDtypeStruct((height, breadth), jnp.bfloat16),
            jax.ShapeDtypeStruct((groups, LANES), jnp.int32),
        ],
        in_specs=[
            pl.BlockSpec((tokens, LANES), lambda at: (0, at)),
            pl.BlockSpec((table_rows // steps, LANES), lambda at: (at, 0)),
            pl.BlockSpec((groups // steps, LANES), lambda at: (at, 0)),
        ],
        out_specs=[
            pl.BlockSpec((LANES, tokens), lambda at: (at, 0)),
            pl.BlockSpec((LANES, breadth), lambda at: (at, 0)),
            pl.BlockSpec((groups // steps, LANES), lambda at: (at, 0)),
        ],
        compiler_params=pltpu.CompilerParams(vmem_limit_bytes=LIMIT),
        cost_estimate=pl.CostEstimate(flops=0, bytes_accessed=8 * height * breadth, transcendentals=0),
        name="prepare",
    )(*[pltpu.with_memory_space_constraint(x, pltpu.HBM) for x in (acts, sign_rows, index_rows)])
    chunks[0], rows = lax.optimization_barrier((chunks[0], rows))
    for distance in range(0, parties, 2):
        chunks[distance + 1] = flipped(chunks[distance], "param", 1)

    sums = pl.pallas_call(
        functools.partial(sketch_kernel, parties, 1.0 / math.sqrt(height * breadth * parties)),
        out_shape=[jax.ShapeDtypeStruct((groups // parties, LANES), jnp.float32)] * outs,
        in_specs=[vmem] * 5 + [pl.BlockSpec(memory_space=pl.ANY)] + [vmem] * parties,
        out_specs=[vmem] * outs,
        scratch_shapes=[
            pltpu.VMEM((2 * table_rows + SUBLANES, LANES), jnp.float32),
            pltpu.VMEM((tokens, breadth), jnp.bfloat16),
            pltpu.VMEM((height, tokens), jnp.bfloat16),
            pltpu.VMEM((height, breadth), jnp.float32),
            pltpu.VMEM((height, breadth), jnp.float32),
            pltpu.VMEM((groups // 2, LANES), jnp.float32),
            pltpu.SMEM((depth, LANES), jnp.int32),
            pltpu.SMEM((depth, LANES), jnp.int32),
            pltpu.SemaphoreType.DMA((2,)),
        ]
        + [pltpu.VMEM((LANES, LANES), jnp.float32)] * depth,
        compiler_params=pltpu.CompilerParams(vmem_limit_bytes=LIMIT),
        name="sketch",
    )(
        turned,
        sign_matrix,
        other_acts,
        other_signs,
        index_rows,
        rows,
        *[chunks[d] for d in range(parties)],
    )

    total = sums[0]
    for out in range(1, outs):
        total = total + flipped(sums[out], "param", 2 * out)
    return total.reshape(1, samples // parties)


def solution(mesh):
    in_specs = (P("ex", None, "param"), P("ex", "param", None), P("param"), P())
    out_specs = P("ex", "param")
    return jax.shard_map(
        on_device, mesh=mesh, in_specs=in_specs, out_specs=out_specs, check_vma=False
    )
```

```python
import functools
import math

import jax
import jax.numpy as jnp
from jax import lax
from jax.experimental import pallas as pl
from jax.experimental.pallas import tpu as pltpu
from jax.sharding import PartitionSpec as P

LANES = 128
LANE_BITS = 7
SIDE = 256
SUBLANES = 8
DEPTH = 16
LIMIT = 24 * 1024 * 1024


def flipped(x, axis, mask):
    return lax.ppermute(x, axis, [(i, i ^ mask) for i in range(lax.axis_size(axis))])


def parity(bits, width):
    shift = 1 << (width - 1).bit_length() >> 1
    while shift:
        bits = bits ^ (bits >> shift)
        shift //= 2
    return bits & 1


def butterfly(parts):
    stride = 1
    while stride < len(parts):
        parts = [
            parts[i] + parts[i + stride] if not i & stride else parts[i - stride] - parts[i]
            for i in range(len(parts))
        ]
        stride *= 2
    return parts


def split(x):
    high = x.astype(jnp.bfloat16)
    return high, (x - high.astype(jnp.float32)).astype(jnp.bfloat16)


def dot(left, right):
    return jnp.dot(left, right, preferred_element_type=jnp.float32)


def prepare_kernel(acts_ref, signs_ref, index_ref, turned_ref, signs_out_ref, rows_ref):
    rows, breadth = signs_out_ref.shape
    spread = breadth // LANES
    for piece in range(spread):
        part = signs_ref[pl.ds(piece, rows, stride=spread), :]
        signs_out_ref[:, piece * LANES : (piece + 1) * LANES] = part.astype(jnp.float32).astype(jnp.bfloat16)
    turned_ref[...] = acts_ref[...].T
    height = rows * pl.num_programs(0)
    index = index_ref[...]
    at_row = ((index >> LANE_BITS) & (spread - 1)) * height + ((index // breadth) & (height - 1))
    half = (index // (breadth * height)) & 1
    rows_ref[...] = half * (spread * height) + at_row


def gather(parties, scale, outs, table, index_ref, rows_hbm, out_refs, scratch):
    result, rows_even, rows_odd, rows_sems, *picked = scratch
    me = lax.axis_index("param")
    share = index_ref.shape[0] // parties
    groups = share * len(outs)
    depth = len(picked)
    last = groups // depth - 1
    singles = table.reshape(table.shape[0], 1, LANES)
    sub_at = lax.broadcasted_iota(jnp.int32, (LANES, LANES), 0)

    def start_of(out):
        return pl.multiple_of((me ^ (2 * out)) * share, share)

    def place(group):
        return start_of(outs[0] + group // share) + group % share

    def fetched(batch, half):
        start = pl.multiple_of(place(jnp.minimum(batch, last) * depth), depth)
        target = (rows_even, rows_odd)[half]
        return pltpu.make_async_copy(rows_hbm.at[pl.ds(start, depth), :], target, rows_sems.at[half])

    def choose(group, rows):
        lane = index_ref[pl.ds(place(group), 1), :] & (LANES - 1)
        chosen = jnp.where(sub_at == lane, rows[...].T, 0.0)
        result[pl.ds(group, 1), :] = jnp.sum(chosen, axis=0, keepdims=True)

    def step(at, carry):
        for half, rows_ref in enumerate((rows_even, rows_odd)):
            batch = 2 * at + half
            first_group = jnp.minimum(batch, last) * depth
            fetched(batch, half).wait()
            for slot in range(depth):
                before = jnp.maximum(batch * depth - 1, 0) if slot == 0 else first_group + slot - 1
                choose(before, picked[slot - 1])
                for first in range(0, LANES, SUBLANES):
                    at_rows = [rows_ref[slot, first + k] for k in range(SUBLANES)]
                    lines = [jnp.broadcast_to(singles[row], (SUBLANES, LANES)) for row in at_rows]
                    merged = lines[0]
                    for k in range(1, SUBLANES):
                        merged = jnp.where(sub_at[:SUBLANES] == k, lines[k], merged)
                    picked[slot][first : first + SUBLANES, :] = merged
            fetched(batch + 2, half).start()
        return carry

    def begin():
        fetched(0, 0).start()
        fetched(1, 1).start()

    def finish():
        lax.fori_loop(0, (last + 2) // 2, step, 0)
        for half in range(2):
            fetched(last, half).wait()
        choose(groups - 1, picked[-1])
        bits = ((table.shape[0] - SUBLANES) // 2 * LANES).bit_length() - 1
        for at, (out, out_ref) in enumerate(zip(outs, out_refs)):
            owner = index_ref[pl.ds(start_of(out), share), :] >> bits
            sign = (1 - 2 * parity(owner & me, parties.bit_length() - 1)).astype(jnp.float32)
            out_ref[...] = result[at * share : (at + 1) * share, :] * (sign * scale)

    return begin, finish


def own_kernel(parties, scale, table, index_ref, rows_hbm, out_ref, *scratch):
    begin, finish = gather(parties, scale, [0], table, index_ref, rows_hbm, [out_ref], scratch)
    begin()
    finish()


def sketch_kernel(parties, scale, own_turned, own_signs, other_acts, other_signs, index_ref, rows_hbm, *refs):
    outs = list(range(1, parties // 2))
    chunk_refs, table, refs = refs[:parties], refs[parties], refs[parties + 1 :]
    out_refs, scratch = refs[: len(outs)], refs[len(outs) :]
    cots, other_turned, total, change, *scratch = scratch
    me = lax.axis_index("param")
    height, breadth = total.shape
    spread = breadth // LANES
    tokens = chunk_refs[0].shape[0]
    begin, finish = gather(parties, scale, outs, table, index_ref, rows_hbm, out_refs, scratch)
    begin()

    for distance in range(parties):
        start = pl.multiple_of((me ^ distance) * tokens, tokens)
        cots[pl.ds(start, tokens), :] = chunk_refs[distance][...]

    row_at = lax.broadcasted_iota(jnp.int32, (SIDE, SIDE), 0)
    col_at = lax.broadcasted_iota(jnp.int32, (SIDE, SIDE), 1)
    hadamard = (1 - 2 * parity(row_at & col_at, 8)).astype(jnp.float32).astype(jnp.bfloat16)

    tall = jnp.concatenate([hadamard, hadamard], axis=0)
    wide = jnp.concatenate([hadamard, hadamard], axis=1)

    row_blocks, col_blocks, pieces = height // SIDE, breadth // SIDE, SIDE // LANES
    for col in range(col_blocks):
        cols = slice(col * SIDE, (col + 1) * SIDE)
        own = dot(own_turned[...], cots[:, cols]) * own_signs[:, cols].astype(jnp.float32)
        if col == 0:
            other_turned[...] = other_acts[...].T
        strips = [other_signs[pl.ds(col * pieces + piece, height, stride=spread), :] for piece in range(pieces)]
        other = dot(other_turned[...], cots[:, cols]) * jnp.concatenate(strips, axis=1).astype(jnp.float32)
        for signed, product in ((total, own + other), (change, own - other)):
            parts = butterfly([product[row * SIDE : (row + 1) * SIDE] for row in range(row_blocks)])
            for row in range(row_blocks):
                signed[row * SIDE : (row + 1) * SIDE, cols] = parts[row]
    for half, signed in enumerate((total, change)):
        for row in range(row_blocks):
            rows = slice(row * SIDE, (row + 1) * SIDE)
            parts = butterfly([signed[rows, col * SIDE : (col + 1) * SIDE] for col in range(col_blocks)])
            for col in range(col_blocks):
                half_done = dot(jnp.concatenate(split(parts[col]), axis=1), tall)
                done = dot(wide, jnp.concatenate(split(half_done), axis=0))
                for piece in range(pieces):
                    at = (half * spread + col * pieces + piece) * height + row * SIDE
                    table[at : at + SIDE, :] = done[:, piece * LANES : (piece + 1) * LANES]

    finish()


def on_device(activations, cotangents, signs, indices):
    tokens, height = activations.shape[1:]
    breadth = cotangents.shape[2]
    parties = lax.axis_size("param")
    samples = indices.shape[0]
    groups = samples // LANES
    table_rows = height * breadth // LANES
    outs = parties // 2
    depth = min(DEPTH, groups // parties)
    vmem = pl.BlockSpec(memory_space=pltpu.VMEM)

    chunks = {0: cotangents[0]}
    for distance in range(2, parties, 2):
        chunks[distance] = flipped(chunks[0], "param", distance)
    acts = activations[0]
    sign_rows = signs.reshape(table_rows, LANES)
    index_rows = indices.reshape(groups, LANES)
    other_acts, other_signs = flipped(acts, "param", 1), flipped(sign_rows, "param", 1)

    steps = height // LANES
    turned, sign_matrix, rows = pl.pallas_call(
        prepare_kernel,
        grid=(steps,),
        out_shape=[
            jax.ShapeDtypeStruct((height, tokens), jnp.bfloat16),
            jax.ShapeDtypeStruct((height, breadth), jnp.bfloat16),
            jax.ShapeDtypeStruct((groups, LANES), jnp.int32),
        ],
        in_specs=[
            pl.BlockSpec((tokens, LANES), lambda at: (0, at)),
            pl.BlockSpec((table_rows // steps, LANES), lambda at: (at, 0)),
            pl.BlockSpec((groups // steps, LANES), lambda at: (at, 0)),
        ],
        out_specs=[
            pl.BlockSpec((LANES, tokens), lambda at: (at, 0)),
            pl.BlockSpec((LANES, breadth), lambda at: (at, 0)),
            pl.BlockSpec((groups // steps, LANES), lambda at: (at, 0)),
        ],
        compiler_params=pltpu.CompilerParams(vmem_limit_bytes=LIMIT),
        cost_estimate=pl.CostEstimate(flops=0, bytes_accessed=8 * height * breadth, transcendentals=0),
        name="prepare",
    )(*[pltpu.with_memory_space_constraint(x, pltpu.HBM) for x in (acts, sign_rows, index_rows)])
    chunks[0], rows = lax.optimization_barrier((chunks[0], rows))
    for distance in range(0, parties, 2):
        chunks[distance + 1] = flipped(chunks[distance], "param", 1)

    scale = 1.0 / math.sqrt(height * breadth * parties)
    block = jax.ShapeDtypeStruct((groups // parties, LANES), jnp.float32)
    any_place = pl.BlockSpec(memory_space=pl.ANY)

    def gather_scratch(blocks):
        return [
            pltpu.VMEM((blocks * (groups // parties), LANES), jnp.float32),
            pltpu.SMEM((depth, LANES), jnp.int32),
            pltpu.SMEM((depth, LANES), jnp.int32),
            pltpu.SemaphoreType.DMA((2,)),
        ] + [pltpu.VMEM((LANES, LANES), jnp.float32)] * depth

    table, *sums = pl.pallas_call(
        functools.partial(sketch_kernel, parties, scale),
        out_shape=[jax.ShapeDtypeStruct((2 * table_rows + SUBLANES, LANES), jnp.float32)] + [block] * (outs - 1),
        in_specs=[vmem] * 5 + [any_place] + [vmem] * parties,
        out_specs=[vmem] * outs,
        scratch_shapes=[
            pltpu.VMEM((tokens, breadth), jnp.bfloat16),
            pltpu.VMEM((height, tokens), jnp.bfloat16),
            pltpu.VMEM((height, breadth), jnp.float32),
            pltpu.VMEM((height, breadth), jnp.float32),
        ]
        + gather_scratch(outs - 1),
        compiler_params=pltpu.CompilerParams(vmem_limit_bytes=LIMIT),
        name="sketch",
    )(
        turned,
        sign_matrix,
        other_acts,
        other_signs,
        index_rows,
        rows,
        *[chunks[d] for d in range(parties)],
    )
    total = pl.pallas_call(
        functools.partial(own_kernel, parties, scale),
        out_shape=block,
        in_specs=[vmem, vmem, any_place],
        out_specs=vmem,
        scratch_shapes=gather_scratch(1),
        compiler_params=pltpu.CompilerParams(vmem_limit_bytes=LIMIT),
        cost_estimate=pl.CostEstimate(flops=0, bytes_accessed=8 * height * breadth, transcendentals=0),
        name="own",
    )(table, index_rows, rows)

    for out in range(1, outs):
        total = total + flipped(sums[out - 1], "param", 2 * out)
    return total.reshape(1, samples // parties)


def solution(mesh):
    in_specs = (P("ex", None, "param"), P("ex", "param", None), P("param"), P())
    out_specs = P("ex", "param")
    return jax.shard_map(
        on_device, mesh=mesh, in_specs=in_specs, out_specs=out_specs, check_vma=False
    )
```

```python
import functools
import math

import jax
import jax.numpy as jnp
from jax import lax
from jax.experimental import pallas as pl
from jax.experimental.pallas import tpu as pltpu
from jax.sharding import PartitionSpec as P

LANES = 128
LANE_BITS = 7
SIDE = 256
SUBLANES = 8
DEPTH = 16
LIMIT = 24 * 1024 * 1024


def flipped(x, axis, mask):
    return lax.ppermute(x, axis, [(i, i ^ mask) for i in range(lax.axis_size(axis))])


def parity(bits, width):
    shift = 1 << (width - 1).bit_length() >> 1
    while shift:
        bits = bits ^ (bits >> shift)
        shift //= 2
    return bits & 1


def butterfly(parts):
    stride = 1
    while stride < len(parts):
        parts = [
            parts[i] + parts[i + stride] if not i & stride else parts[i - stride] - parts[i]
            for i in range(len(parts))
        ]
        stride *= 2
    return parts


def split(x):
    high = x.astype(jnp.bfloat16)
    return high, (x - high.astype(jnp.float32)).astype(jnp.bfloat16)


def dot(left, right):
    return jnp.dot(left, right, preferred_element_type=jnp.float32)


def prepare_kernel(acts_ref, signs_ref, index_ref, turned_ref, signs_out_ref, rows_ref):
    rows, breadth = signs_out_ref.shape
    spread = breadth // LANES
    for piece in range(spread):
        part = signs_ref[pl.ds(piece, rows, stride=spread), :]
        signs_out_ref[:, piece * LANES : (piece + 1) * LANES] = part.astype(jnp.float32).astype(jnp.bfloat16)
    turned_ref[...] = acts_ref[...].T
    height = rows * pl.num_programs(0)
    index = index_ref[...]
    at_row = ((index >> LANE_BITS) & (spread - 1)) * height + ((index // breadth) & (height - 1))
    half = (index // (breadth * height)) & 1
    rows_ref[...] = half * (spread * height) + at_row


def gather(parties, scale, outs, table, index_ref, rows_hbm, out_refs, scratch):
    result, rows_even, rows_odd, rows_sems, *picked = scratch
    me = lax.axis_index("param")
    share = index_ref.shape[0] // parties
    groups = share * len(outs)
    depth = len(picked)
    last = groups // depth - 1
    singles = table.reshape(table.shape[0], 1, LANES)
    sub_at = lax.broadcasted_iota(jnp.int32, (LANES, LANES), 0)

    def start_of(out):
        return pl.multiple_of((me ^ (2 * out)) * share, share)

    def place(group):
        return start_of(outs[0] + group // share) + group % share

    def fetched(batch, half):
        start = pl.multiple_of(place(jnp.minimum(batch, last) * depth), depth)
        target = (rows_even, rows_odd)[half]
        return pltpu.make_async_copy(rows_hbm.at[pl.ds(start, depth), :], target, rows_sems.at[half])

    def choose(group, rows):
        lane = index_ref[pl.ds(place(group), 1), :] & (LANES - 1)
        chosen = jnp.where(sub_at == lane, rows[...].T, 0.0)
        result[pl.ds(group, 1), :] = jnp.sum(chosen, axis=0, keepdims=True)

    def step(at, carry):
        for half, rows_ref in enumerate((rows_even, rows_odd)):
            batch = 2 * at + half
            first_group = jnp.minimum(batch, last) * depth
            fetched(batch, half).wait()
            for slot in range(depth):
                before = jnp.maximum(batch * depth - 1, 0) if slot == 0 else first_group + slot - 1
                choose(before, picked[slot - 1])
                for first in range(0, LANES, SUBLANES):
                    at_rows = [rows_ref[slot, first + k] for k in range(SUBLANES)]
                    lines = [jnp.broadcast_to(singles[row], (SUBLANES, LANES)) for row in at_rows]
                    merged = lines[0]
                    for k in range(1, SUBLANES):
                        merged = jnp.where(sub_at[:SUBLANES] == k, lines[k], merged)
                    picked[slot][first : first + SUBLANES, :] = merged
            fetched(batch + 2, half).start()
        return carry

    def begin():
        fetched(0, 0).start()
        fetched(1, 1).start()

    def finish():
        lax.fori_loop(0, (last + 2) // 2, step, 0)
        for half in range(2):
            fetched(last, half).wait()
        choose(groups - 1, picked[-1])
        bits = ((table.shape[0] - SUBLANES) // 2 * LANES).bit_length() - 1
        for at, (out, out_ref) in enumerate(zip(outs, out_refs)):
            owner = index_ref[pl.ds(start_of(out), share), :] >> bits
            sign = (1 - 2 * parity(owner & me, parties.bit_length() - 1)).astype(jnp.float32)
            out_ref[...] = result[at * share : (at + 1) * share, :] * (sign * scale)

    return begin, finish


def own_kernel(parties, scale, table, index_ref, rows_hbm, out_ref, *scratch):
    begin, finish = gather(parties, scale, [0], table, index_ref, rows_hbm, [out_ref], scratch)
    begin()
    finish()


def sketch_kernel(parties, scale, own_turned, own_signs, other_acts, other_signs, index_ref, rows_hbm, *refs):
    outs = list(range(1, parties // 2))
    chunk_refs, table, refs = refs[:parties], refs[parties], refs[parties + 1 :]
    out_refs, scratch = refs[: len(outs)], refs[len(outs) :]
    cots, other_turned, total, change, *scratch = scratch
    me = lax.axis_index("param")
    height, breadth = total.shape
    spread = breadth // LANES
    tokens = chunk_refs[0].shape[0]
    begin, finish = gather(parties, scale, outs, table, index_ref, rows_hbm, out_refs, scratch)
    begin()

    for distance in range(parties):
        start = pl.multiple_of((me ^ distance) * tokens, tokens)
        cots[pl.ds(start, tokens), :] = chunk_refs[distance][...]

    row_at = lax.broadcasted_iota(jnp.int32, (SIDE, SIDE), 0)
    col_at = lax.broadcasted_iota(jnp.int32, (SIDE, SIDE), 1)
    hadamard = (1 - 2 * parity(row_at & col_at, 8)).astype(jnp.float32).astype(jnp.bfloat16)

    tall = jnp.concatenate([hadamard, hadamard], axis=0)
    wide = jnp.concatenate([hadamard, hadamard], axis=1)

    row_blocks, col_blocks, pieces = height // SIDE, breadth // SIDE, SIDE // LANES
    for col in range(col_blocks):
        cols = slice(col * SIDE, (col + 1) * SIDE)
        own = dot(own_turned[...], cots[:, cols]) * own_signs[:, cols].astype(jnp.float32)
        if col == 0:
            other_turned[...] = other_acts[...].T
        strips = [other_signs[pl.ds(col * pieces + piece, height, stride=spread), :] for piece in range(pieces)]
        other = dot(other_turned[...], cots[:, cols]) * jnp.concatenate(strips, axis=1).astype(jnp.float32)
        for signed, product in ((total, own + other), (change, own - other)):
            parts = butterfly([product[row * SIDE : (row + 1) * SIDE] for row in range(row_blocks)])
            for row in range(row_blocks):
                signed[row * SIDE : (row + 1) * SIDE, cols] = parts[row]
    for half, signed in enumerate((total, change)):
        for row in range(row_blocks):
            rows = slice(row * SIDE, (row + 1) * SIDE)
            parts = butterfly([signed[rows, col * SIDE : (col + 1) * SIDE] for col in range(col_blocks)])
            stacked = jnp.concatenate(parts, axis=0)
            high, low = split(dot(jnp.concatenate(split(stacked), axis=1), tall))
            for col in range(col_blocks):
                block = slice(col * SIDE, (col + 1) * SIDE)
                done = dot(wide, jnp.concatenate([high[block], low[block]], axis=0))
                for piece in range(pieces):
                    at = (half * spread + col * pieces + piece) * height + row * SIDE
                    table[at : at + SIDE, :] = done[:, piece * LANES : (piece + 1) * LANES]

    finish()


def on_device(activations, cotangents, signs, indices):
    tokens, height = activations.shape[1:]
    breadth = cotangents.shape[2]
    parties = lax.axis_size("param")
    samples = indices.shape[0]
    groups = samples // LANES
    table_rows = height * breadth // LANES
    outs = parties // 2
    depth = min(DEPTH, groups // parties)
    vmem = pl.BlockSpec(memory_space=pltpu.VMEM)

    chunks = {0: cotangents[0]}
    for distance in range(2, parties, 2):
        chunks[distance] = flipped(chunks[0], "param", distance)
    acts = activations[0]
    sign_rows = signs.reshape(table_rows, LANES)
    index_rows = indices.reshape(groups, LANES)
    other_acts, other_signs = flipped(acts, "param", 1), flipped(sign_rows, "param", 1)

    steps = height // LANES
    turned, sign_matrix, rows = pl.pallas_call(
        prepare_kernel,
        grid=(steps,),
        out_shape=[
            jax.ShapeDtypeStruct((height, tokens), jnp.bfloat16),
            jax.ShapeDtypeStruct((height, breadth), jnp.bfloat16),
            jax.ShapeDtypeStruct((groups, LANES), jnp.int32),
        ],
        in_specs=[
            pl.BlockSpec((tokens, LANES), lambda at: (0, at)),
            pl.BlockSpec((table_rows // steps, LANES), lambda at: (at, 0)),
            pl.BlockSpec((groups // steps, LANES), lambda at: (at, 0)),
        ],
        out_specs=[
            pl.BlockSpec((LANES, tokens), lambda at: (at, 0)),
            pl.BlockSpec((LANES, breadth), lambda at: (at, 0)),
            pl.BlockSpec((groups // steps, LANES), lambda at: (at, 0)),
        ],
        compiler_params=pltpu.CompilerParams(vmem_limit_bytes=LIMIT),
        cost_estimate=pl.CostEstimate(flops=0, bytes_accessed=8 * height * breadth, transcendentals=0),
        name="prepare",
    )(*[pltpu.with_memory_space_constraint(x, pltpu.HBM) for x in (acts, sign_rows, index_rows)])
    chunks[0], rows = lax.optimization_barrier((chunks[0], rows))
    for distance in range(0, parties, 2):
        chunks[distance + 1] = flipped(chunks[distance], "param", 1)

    scale = 1.0 / math.sqrt(height * breadth * parties)
    block = jax.ShapeDtypeStruct((groups // parties, LANES), jnp.float32)
    any_place = pl.BlockSpec(memory_space=pl.ANY)

    def gather_scratch(blocks):
        return [
            pltpu.VMEM((blocks * (groups // parties), LANES), jnp.float32),
            pltpu.SMEM((depth, LANES), jnp.int32),
            pltpu.SMEM((depth, LANES), jnp.int32),
            pltpu.SemaphoreType.DMA((2,)),
        ] + [pltpu.VMEM((LANES, LANES), jnp.float32)] * depth

    table, *sums = pl.pallas_call(
        functools.partial(sketch_kernel, parties, scale),
        out_shape=[jax.ShapeDtypeStruct((2 * table_rows + SUBLANES, LANES), jnp.float32)] + [block] * (outs - 1),
        in_specs=[vmem] * 5 + [any_place] + [vmem] * parties,
        out_specs=[vmem] * outs,
        scratch_shapes=[
            pltpu.VMEM((tokens, breadth), jnp.bfloat16),
            pltpu.VMEM((height, tokens), jnp.bfloat16),
            pltpu.VMEM((height, breadth), jnp.float32),
            pltpu.VMEM((height, breadth), jnp.float32),
        ]
        + gather_scratch(outs - 1),
        compiler_params=pltpu.CompilerParams(vmem_limit_bytes=LIMIT),
        name="sketch",
    )(
        turned,
        sign_matrix,
        other_acts,
        other_signs,
        index_rows,
        rows,
        *[chunks[d] for d in range(parties)],
    )
    total = pl.pallas_call(
        functools.partial(own_kernel, parties, scale),
        out_shape=block,
        in_specs=[vmem, vmem, any_place],
        out_specs=vmem,
        scratch_shapes=gather_scratch(1),
        compiler_params=pltpu.CompilerParams(vmem_limit_bytes=LIMIT),
        cost_estimate=pl.CostEstimate(flops=0, bytes_accessed=8 * height * breadth, transcendentals=0),
        name="own",
    )(table, index_rows, rows)

    for out in range(1, outs):
        total = total + flipped(sums[out - 1], "param", 2 * out)
    return total.reshape(1, samples // parties)


def solution(mesh):
    in_specs = (P("ex", None, "param"), P("ex", "param", None), P("param"), P())
    out_specs = P("ex", "param")
    return jax.shard_map(
        on_device, mesh=mesh, in_specs=in_specs, out_specs=out_specs, check_vma=False
    )
```

```python
import functools
import math

import jax
import jax.numpy as jnp
from jax import lax
from jax.experimental import pallas as pl
from jax.experimental.pallas import tpu as pltpu
from jax.sharding import PartitionSpec as P

LANES = 128
LANE_BITS = 7
SIDE = 256
SUBLANES = 8
DEPTH = 16
LIMIT = 24 * 1024 * 1024


def flipped(x, axis, mask):
    return lax.ppermute(x, axis, [(i, i ^ mask) for i in range(lax.axis_size(axis))])


def parity(bits, width):
    shift = 1 << (width - 1).bit_length() >> 1
    while shift:
        bits = bits ^ (bits >> shift)
        shift //= 2
    return bits & 1


def butterfly(parts):
    stride = 1
    while stride < len(parts):
        parts = [
            parts[i] + parts[i + stride] if not i & stride else parts[i - stride] - parts[i]
            for i in range(len(parts))
        ]
        stride *= 2
    return parts


def split(x):
    high = x.astype(jnp.bfloat16)
    return high, (x - high.astype(jnp.float32)).astype(jnp.bfloat16)


def dot(left, right):
    return jnp.dot(left, right, preferred_element_type=jnp.float32)


def prepare_kernel(acts_hbm, signs_hbm, index_hbm, turned_ref, signs_out_ref, rows_ref, acts_ref, signs_ref, index_ref, sems):
    height, breadth = signs_out_ref.shape
    spread = breadth // LANES
    index_load = pltpu.make_async_copy(index_hbm, index_ref, sems.at[0])
    sign_loads, acts_loads = [], []
    for at in range(height // LANES):
        piece = pl.ds(at * LANES * spread, LANES * spread)
        sign_loads.append(pltpu.make_async_copy(signs_hbm.at[piece, :], signs_ref.at[piece, :], sems.at[1 + at]))
    for at in range(height // SIDE):
        piece = pl.ds(at * SIDE, SIDE)
        sem = sems.at[1 + height // LANES + at]
        acts_loads.append(pltpu.make_async_copy(acts_hbm.at[:, piece], acts_ref.at[:, piece], sem))
    for load in [index_load] + sign_loads + acts_loads:
        load.start()

    index_load.wait()
    index = index_ref[...]
    at_row = ((index >> LANE_BITS) & (spread - 1)) * height + ((index // breadth) & (height - 1))
    half = (index // (breadth * height)) & 1
    rows_ref[...] = half * (spread * height) + at_row
    for at, load in enumerate(sign_loads):
        load.wait()
        for strip in range(spread):
            part = signs_ref[pl.ds(at * LANES * spread + strip, LANES, stride=spread), :]
            part = part.astype(jnp.float32).astype(jnp.bfloat16)
            signs_out_ref[at * LANES : (at + 1) * LANES, strip * LANES : (strip + 1) * LANES] = part
    for at, load in enumerate(acts_loads):
        load.wait()
        turned_ref[at * SIDE : (at + 1) * SIDE, :] = acts_ref[:, at * SIDE : (at + 1) * SIDE].T


def gather(parties, scale, outs, table, index_ref, rows_hbm, out_refs, scratch):
    result, rows_even, rows_odd, rows_sems, *picked = scratch
    me = lax.axis_index("param")
    share = index_ref.shape[0] // parties
    groups = share * len(outs)
    depth = len(picked)
    last = groups // depth - 1
    singles = table.reshape(table.shape[0], 1, LANES)
    sub_at = lax.broadcasted_iota(jnp.int32, (LANES, LANES), 0)

    def start_of(out):
        return pl.multiple_of((me ^ (2 * out)) * share, share)

    def place(group):
        return start_of(outs[0] + group // share) + group % share

    def fetched(batch, half):
        start = pl.multiple_of(place(jnp.minimum(batch, last) * depth), depth)
        target = (rows_even, rows_odd)[half]
        return pltpu.make_async_copy(rows_hbm.at[pl.ds(start, depth), :], target, rows_sems.at[half])

    def choose(group, rows):
        lane = index_ref[pl.ds(place(group), 1), :] & (LANES - 1)
        chosen = jnp.where(sub_at == lane, rows[...].T, 0.0)
        result[pl.ds(group, 1), :] = jnp.sum(chosen, axis=0, keepdims=True)

    def step(at, carry):
        for half, rows_ref in enumerate((rows_even, rows_odd)):
            batch = 2 * at + half
            first_group = jnp.minimum(batch, last) * depth
            fetched(batch, half).wait()
            for slot in range(depth):
                before = jnp.maximum(batch * depth - 1, 0) if slot == 0 else first_group + slot - 1
                choose(before, picked[slot - 1])
                for first in range(0, LANES, SUBLANES):
                    at_rows = [rows_ref[slot, first + k] for k in range(SUBLANES)]
                    lines = [jnp.broadcast_to(singles[row], (SUBLANES, LANES)) for row in at_rows]
                    merged = lines[0]
                    for k in range(1, SUBLANES):
                        merged = jnp.where(sub_at[:SUBLANES] == k, lines[k], merged)
                    picked[slot][first : first + SUBLANES, :] = merged
            fetched(batch + 2, half).start()
        return carry

    def begin():
        fetched(0, 0).start()
        fetched(1, 1).start()

    def finish():
        lax.fori_loop(0, (last + 2) // 2, step, 0)
        for half in range(2):
            fetched(last, half).wait()
        choose(groups - 1, picked[-1])
        bits = ((table.shape[0] - SUBLANES) // 2 * LANES).bit_length() - 1
        for at, (out, out_ref) in enumerate(zip(outs, out_refs)):
            owner = index_ref[pl.ds(start_of(out), share), :] >> bits
            sign = (1 - 2 * parity(owner & me, parties.bit_length() - 1)).astype(jnp.float32)
            out_ref[...] = result[at * share : (at + 1) * share, :] * (sign * scale)

    return begin, finish


def own_kernel(parties, scale, table, index_ref, rows_hbm, out_ref, *scratch):
    begin, finish = gather(parties, scale, [0], table, index_ref, rows_hbm, [out_ref], scratch)
    begin()
    finish()


def sketch_kernel(parties, scale, own_turned, own_signs, other_acts, other_signs, index_ref, rows_hbm, *refs):
    outs = list(range(1, parties // 2))
    chunk_refs, table, refs = refs[:parties], refs[parties], refs[parties + 1 :]
    out_refs, scratch = refs[: len(outs)], refs[len(outs) :]
    cots, other_turned, total, change, *scratch = scratch
    me = lax.axis_index("param")
    height, breadth = total.shape
    spread = breadth // LANES
    tokens = chunk_refs[0].shape[0]
    begin, finish = gather(parties, scale, outs, table, index_ref, rows_hbm, out_refs, scratch)
    begin()

    for distance in range(parties):
        start = pl.multiple_of((me ^ distance) * tokens, tokens)
        cots[pl.ds(start, tokens), :] = chunk_refs[distance][...]

    row_at = lax.broadcasted_iota(jnp.int32, (SIDE, SIDE), 0)
    col_at = lax.broadcasted_iota(jnp.int32, (SIDE, SIDE), 1)
    hadamard = (1 - 2 * parity(row_at & col_at, 8)).astype(jnp.float32).astype(jnp.bfloat16)

    tall = jnp.concatenate([hadamard, hadamard], axis=0)
    wide = jnp.concatenate([hadamard, hadamard], axis=1)

    row_blocks, col_blocks, pieces = height // SIDE, breadth // SIDE, SIDE // LANES
    for col in range(col_blocks):
        cols = slice(col * SIDE, (col + 1) * SIDE)
        own = dot(own_turned[...], cots[:, cols]) * own_signs[:, cols].astype(jnp.float32)
        if col == 0:
            other_turned[...] = other_acts[...].T
        strips = [other_signs[pl.ds(col * pieces + piece, height, stride=spread), :] for piece in range(pieces)]
        other = dot(other_turned[...], cots[:, cols]) * jnp.concatenate(strips, axis=1).astype(jnp.float32)
        for signed, product in ((total, own + other), (change, own - other)):
            parts = butterfly([product[row * SIDE : (row + 1) * SIDE] for row in range(row_blocks)])
            for row in range(row_blocks):
                signed[row * SIDE : (row + 1) * SIDE, cols] = parts[row]
    for half, signed in enumerate((total, change)):
        for row in range(row_blocks):
            rows = slice(row * SIDE, (row + 1) * SIDE)
            parts = butterfly([signed[rows, col * SIDE : (col + 1) * SIDE] for col in range(col_blocks)])
            for col in range(col_blocks):
                half_done = dot(jnp.concatenate(split(parts[col]), axis=1), tall)
                done = dot(wide, jnp.concatenate(split(half_done), axis=0))
                for piece in range(pieces):
                    at = (half * spread + col * pieces + piece) * height + row * SIDE
                    table[at : at + SIDE, :] = done[:, piece * LANES : (piece + 1) * LANES]

    finish()


def on_device(activations, cotangents, signs, indices):
    tokens, height = activations.shape[1:]
    breadth = cotangents.shape[2]
    parties = lax.axis_size("param")
    samples = indices.shape[0]
    groups = samples // LANES
    table_rows = height * breadth // LANES
    outs = parties // 2
    depth = min(DEPTH, groups // parties)
    vmem = pl.BlockSpec(memory_space=pltpu.VMEM)

    chunks = {0: cotangents[0]}
    for distance in range(2, parties, 2):
        chunks[distance] = flipped(chunks[0], "param", distance)
    acts = activations[0]
    sign_rows = signs.reshape(table_rows, LANES)
    index_rows = indices.reshape(groups, LANES)
    other_acts, other_signs = flipped(acts, "param", 1), flipped(sign_rows, "param", 1)

    turned, sign_matrix, rows = pl.pallas_call(
        prepare_kernel,
        out_shape=[
            jax.ShapeDtypeStruct((height, tokens), jnp.bfloat16),
            jax.ShapeDtypeStruct((height, breadth), jnp.bfloat16),
            jax.ShapeDtypeStruct((groups, LANES), jnp.int32),
        ],
        in_specs=[pl.BlockSpec(memory_space=pl.ANY)] * 3,
        out_specs=[vmem] * 3,
        scratch_shapes=[
            pltpu.VMEM((tokens, height), jnp.bfloat16),
            pltpu.VMEM((table_rows, LANES), jnp.int32),
            pltpu.VMEM((groups, LANES), jnp.int32),
            pltpu.SemaphoreType.DMA((1 + height // LANES + height // SIDE,)),
        ],
        compiler_params=pltpu.CompilerParams(vmem_limit_bytes=LIMIT),
        cost_estimate=pl.CostEstimate(flops=0, bytes_accessed=8 * height * breadth, transcendentals=0),
        name="prepare",
    )(*[pltpu.with_memory_space_constraint(x, pltpu.HBM) for x in (acts, sign_rows, index_rows)])
    chunks[0], rows = lax.optimization_barrier((chunks[0], rows))
    for distance in range(0, parties, 2):
        chunks[distance + 1] = flipped(chunks[distance], "param", 1)

    scale = 1.0 / math.sqrt(height * breadth * parties)
    block = jax.ShapeDtypeStruct((groups // parties, LANES), jnp.float32)
    any_place = pl.BlockSpec(memory_space=pl.ANY)

    def gather_scratch(blocks):
        return [
            pltpu.VMEM((blocks * (groups // parties), LANES), jnp.float32),
            pltpu.SMEM((depth, LANES), jnp.int32),
            pltpu.SMEM((depth, LANES), jnp.int32),
            pltpu.SemaphoreType.DMA((2,)),
        ] + [pltpu.VMEM((LANES, LANES), jnp.float32)] * depth

    table, *sums = pl.pallas_call(
        functools.partial(sketch_kernel, parties, scale),
        out_shape=[jax.ShapeDtypeStruct((2 * table_rows + SUBLANES, LANES), jnp.float32)] + [block] * (outs - 1),
        in_specs=[vmem] * 5 + [any_place] + [vmem] * parties,
        out_specs=[vmem] * outs,
        scratch_shapes=[
            pltpu.VMEM((tokens, breadth), jnp.bfloat16),
            pltpu.VMEM((height, tokens), jnp.bfloat16),
            pltpu.VMEM((height, breadth), jnp.float32),
            pltpu.VMEM((height, breadth), jnp.float32),
        ]
        + gather_scratch(outs - 1),
        compiler_params=pltpu.CompilerParams(vmem_limit_bytes=LIMIT),
        name="sketch",
    )(
        turned,
        sign_matrix,
        other_acts,
        other_signs,
        index_rows,
        rows,
        *[chunks[d] for d in range(parties)],
    )
    total = pl.pallas_call(
        functools.partial(own_kernel, parties, scale),
        out_shape=block,
        in_specs=[vmem, vmem, any_place],
        out_specs=vmem,
        scratch_shapes=gather_scratch(1),
        compiler_params=pltpu.CompilerParams(vmem_limit_bytes=LIMIT),
        cost_estimate=pl.CostEstimate(flops=0, bytes_accessed=8 * height * breadth, transcendentals=0),
        name="own",
    )(table, index_rows, rows)

    for out in range(1, outs):
        total = total + flipped(sums[out - 1], "param", 2 * out)
    return total.reshape(1, samples // parties)


def solution(mesh):
    in_specs = (P("ex", None, "param"), P("ex", "param", None), P("param"), P())
    out_specs = P("ex", "param")
    return jax.shard_map(
        on_device, mesh=mesh, in_specs=in_specs, out_specs=out_specs, check_vma=False
    )
```

```python
import functools
import math

import jax
import jax.numpy as jnp
from jax import lax
from jax.experimental import pallas as pl
from jax.experimental.pallas import tpu as pltpu
from jax.sharding import PartitionSpec as P

LANES = 128
LANE_BITS = 7
SIDE = 256
SUBLANES = 8
DEPTH = 16
LIMIT = 24 * 1024 * 1024


def flipped(x, axis, mask):
    return lax.ppermute(x, axis, [(i, i ^ mask) for i in range(lax.axis_size(axis))])


def parity(bits, width):
    shift = 1 << (width - 1).bit_length() >> 1
    while shift:
        bits = bits ^ (bits >> shift)
        shift //= 2
    return bits & 1


def butterfly(parts):
    stride = 1
    while stride < len(parts):
        parts = [
            parts[i] + parts[i + stride] if not i & stride else parts[i - stride] - parts[i]
            for i in range(len(parts))
        ]
        stride *= 2
    return parts


def split(x):
    high = x.astype(jnp.bfloat16)
    return high, (x - high.astype(jnp.float32)).astype(jnp.bfloat16)


def dot(left, right):
    return jnp.dot(left, right, preferred_element_type=jnp.float32)


def prepare_kernel(other_acts, acts_hbm, signs_hbm, index_hbm, *refs):
    other_turned, turned_ref, signs_out_ref, rows_ref, acts_ref, signs_ref, index_ref, sems = refs
    height, breadth = signs_out_ref.shape
    spread = breadth // LANES
    index_load = pltpu.make_async_copy(index_hbm, index_ref, sems.at[0])
    sign_loads, acts_loads = [], []
    for at in range(height // LANES):
        piece = pl.ds(at * LANES * spread, LANES * spread)
        sign_loads.append(pltpu.make_async_copy(signs_hbm.at[piece, :], signs_ref.at[piece, :], sems.at[1 + at]))
    for at in range(height // SIDE):
        piece = pl.ds(at * SIDE, SIDE)
        sem = sems.at[1 + height // LANES + at]
        acts_loads.append(pltpu.make_async_copy(acts_hbm.at[:, piece], acts_ref.at[:, piece], sem))
    for load in [index_load] + sign_loads + acts_loads:
        load.start()

    other_turned[...] = other_acts[...].T
    index_load.wait()
    index = index_ref[...]
    at_row = ((index >> LANE_BITS) & (spread - 1)) * height + ((index // breadth) & (height - 1))
    half = (index // (breadth * height)) & 1
    rows_ref[...] = half * (spread * height) + at_row
    for at, load in enumerate(sign_loads):
        load.wait()
        for strip in range(spread):
            part = signs_ref[pl.ds(at * LANES * spread + strip, LANES, stride=spread), :]
            part = part.astype(jnp.float32).astype(jnp.bfloat16)
            signs_out_ref[at * LANES : (at + 1) * LANES, strip * LANES : (strip + 1) * LANES] = part
    for at, load in enumerate(acts_loads):
        load.wait()
        turned_ref[at * SIDE : (at + 1) * SIDE, :] = acts_ref[:, at * SIDE : (at + 1) * SIDE].T


def gather(parties, scale, outs, table, index_ref, rows_hbm, out_refs, scratch):
    result, rows_even, rows_odd, rows_sems, *picked = scratch
    me = lax.axis_index("param")
    share = index_ref.shape[0] // parties
    groups = share * len(outs)
    depth = len(picked)
    last = groups // depth - 1
    singles = table.reshape(table.shape[0], 1, LANES)
    sub_at = lax.broadcasted_iota(jnp.int32, (LANES, LANES), 0)

    def start_of(out):
        return pl.multiple_of((me ^ (2 * out)) * share, share)

    def place(group):
        return start_of(outs[0] + group // share) + group % share

    def fetched(batch, half):
        start = pl.multiple_of(place(jnp.minimum(batch, last) * depth), depth)
        target = (rows_even, rows_odd)[half]
        return pltpu.make_async_copy(rows_hbm.at[pl.ds(start, depth), :], target, rows_sems.at[half])

    def choose(group, rows):
        lane = index_ref[pl.ds(place(group), 1), :] & (LANES - 1)
        chosen = jnp.where(sub_at == lane, rows[...].T, 0.0)
        result[pl.ds(group, 1), :] = jnp.sum(chosen, axis=0, keepdims=True)

    def step(at, carry):
        for half, rows_ref in enumerate((rows_even, rows_odd)):
            batch = 2 * at + half
            first_group = jnp.minimum(batch, last) * depth
            fetched(batch, half).wait()
            for slot in range(depth):
                before = jnp.maximum(batch * depth - 1, 0) if slot == 0 else first_group + slot - 1
                choose(before, picked[slot - 1])
                for first in range(0, LANES, SUBLANES):
                    at_rows = [rows_ref[slot, first + k] for k in range(SUBLANES)]
                    lines = [jnp.broadcast_to(singles[row], (SUBLANES, LANES)) for row in at_rows]
                    merged = lines[0]
                    for k in range(1, SUBLANES):
                        merged = jnp.where(sub_at[:SUBLANES] == k, lines[k], merged)
                    picked[slot][first : first + SUBLANES, :] = merged
            fetched(batch + 2, half).start()
        return carry

    def begin():
        fetched(0, 0).start()
        fetched(1, 1).start()

    def finish():
        lax.fori_loop(0, (last + 2) // 2, step, 0)
        for half in range(2):
            fetched(last, half).wait()
        choose(groups - 1, picked[-1])
        bits = ((table.shape[0] - SUBLANES) // 2 * LANES).bit_length() - 1
        for at, (out, out_ref) in enumerate(zip(outs, out_refs)):
            owner = index_ref[pl.ds(start_of(out), share), :] >> bits
            sign = (1 - 2 * parity(owner & me, parties.bit_length() - 1)).astype(jnp.float32)
            out_ref[...] = result[at * share : (at + 1) * share, :] * (sign * scale)

    return begin, finish


def own_kernel(parties, scale, table, index_ref, rows_hbm, out_ref, *scratch):
    begin, finish = gather(parties, scale, [0], table, index_ref, rows_hbm, [out_ref], scratch)
    begin()
    finish()


def sketch_kernel(parties, scale, own_turned, own_signs, other_turned, other_signs, index_ref, rows_hbm, *refs):
    outs = list(range(1, parties // 2))
    chunk_refs, table, refs = refs[:parties], refs[parties], refs[parties + 1 :]
    out_refs, scratch = refs[: len(outs)], refs[len(outs) :]
    cots, total, change, *scratch = scratch
    me = lax.axis_index("param")
    height, breadth = total.shape
    spread = breadth // LANES
    tokens = chunk_refs[0].shape[0]
    begin, finish = gather(parties, scale, outs, table, index_ref, rows_hbm, out_refs, scratch)
    begin()

    for distance in range(parties):
        start = pl.multiple_of((me ^ distance) * tokens, tokens)
        cots[pl.ds(start, tokens), :] = chunk_refs[distance][...]

    row_at = lax.broadcasted_iota(jnp.int32, (SIDE, SIDE), 0)
    col_at = lax.broadcasted_iota(jnp.int32, (SIDE, SIDE), 1)
    hadamard = (1 - 2 * parity(row_at & col_at, 8)).astype(jnp.float32).astype(jnp.bfloat16)

    tall = jnp.concatenate([hadamard, hadamard], axis=0)
    wide = jnp.concatenate([hadamard, hadamard], axis=1)

    row_blocks, col_blocks, pieces = height // SIDE, breadth // SIDE, SIDE // LANES
    for col in range(col_blocks):
        cols = slice(col * SIDE, (col + 1) * SIDE)
        own = dot(own_turned[...], cots[:, cols]) * own_signs[:, cols].astype(jnp.float32)
        strips = [other_signs[pl.ds(col * pieces + piece, height, stride=spread), :] for piece in range(pieces)]
        other = dot(other_turned[...], cots[:, cols]) * jnp.concatenate(strips, axis=1).astype(jnp.float32)
        for signed, product in ((total, own + other), (change, own - other)):
            parts = butterfly([product[row * SIDE : (row + 1) * SIDE] for row in range(row_blocks)])
            for row in range(row_blocks):
                signed[row * SIDE : (row + 1) * SIDE, cols] = parts[row]
    for half, signed in enumerate((total, change)):
        for row in range(row_blocks):
            rows = slice(row * SIDE, (row + 1) * SIDE)
            parts = butterfly([signed[rows, col * SIDE : (col + 1) * SIDE] for col in range(col_blocks)])
            for col in range(col_blocks):
                half_done = dot(jnp.concatenate(split(parts[col]), axis=1), tall)
                done = dot(wide, jnp.concatenate(split(half_done), axis=0))
                for piece in range(pieces):
                    at = (half * spread + col * pieces + piece) * height + row * SIDE
                    table[at : at + SIDE, :] = done[:, piece * LANES : (piece + 1) * LANES]

    finish()


def on_device(activations, cotangents, signs, indices):
    tokens, height = activations.shape[1:]
    breadth = cotangents.shape[2]
    parties = lax.axis_size("param")
    samples = indices.shape[0]
    groups = samples // LANES
    table_rows = height * breadth // LANES
    outs = parties // 2
    depth = min(DEPTH, groups // parties)
    vmem = pl.BlockSpec(memory_space=pltpu.VMEM)

    chunks = {0: cotangents[0]}
    for distance in range(2, parties, 2):
        chunks[distance] = flipped(chunks[0], "param", distance)
    acts = activations[0]
    sign_rows = signs.reshape(table_rows, LANES)
    index_rows = indices.reshape(groups, LANES)
    other_acts, other_signs = flipped(acts, "param", 1), flipped(sign_rows, "param", 1)

    other_turned, turned, sign_matrix, rows = pl.pallas_call(
        prepare_kernel,
        out_shape=[
            jax.ShapeDtypeStruct((height, tokens), jnp.bfloat16),
            jax.ShapeDtypeStruct((height, tokens), jnp.bfloat16),
            jax.ShapeDtypeStruct((height, breadth), jnp.bfloat16),
            jax.ShapeDtypeStruct((groups, LANES), jnp.int32),
        ],
        in_specs=[vmem] + [pl.BlockSpec(memory_space=pl.ANY)] * 3,
        out_specs=[vmem] * 4,
        scratch_shapes=[
            pltpu.VMEM((tokens, height), jnp.bfloat16),
            pltpu.VMEM((table_rows, LANES), jnp.int32),
            pltpu.VMEM((groups, LANES), jnp.int32),
            pltpu.SemaphoreType.DMA((1 + height // LANES + height // SIDE,)),
        ],
        compiler_params=pltpu.CompilerParams(vmem_limit_bytes=LIMIT),
        cost_estimate=pl.CostEstimate(flops=0, bytes_accessed=8 * height * breadth, transcendentals=0),
        name="prepare",
    )(other_acts, *[pltpu.with_memory_space_constraint(x, pltpu.HBM) for x in (acts, sign_rows, index_rows)])
    held = list(range(0, parties, 2))
    rows, *passed = lax.optimization_barrier((rows, *[chunks[d] for d in held]))
    chunks.update(zip(held, passed))
    for distance in range(0, parties, 2):
        chunks[distance + 1] = flipped(chunks[distance], "param", 1)

    scale = 1.0 / math.sqrt(height * breadth * parties)
    block = jax.ShapeDtypeStruct((groups // parties, LANES), jnp.float32)
    any_place = pl.BlockSpec(memory_space=pl.ANY)

    def gather_scratch(blocks):
        return [
            pltpu.VMEM((blocks * (groups // parties), LANES), jnp.float32),
            pltpu.SMEM((depth, LANES), jnp.int32),
            pltpu.SMEM((depth, LANES), jnp.int32),
            pltpu.SemaphoreType.DMA((2,)),
        ] + [pltpu.VMEM((LANES, LANES), jnp.float32)] * depth

    table, *sums = pl.pallas_call(
        functools.partial(sketch_kernel, parties, scale),
        out_shape=[jax.ShapeDtypeStruct((2 * table_rows + SUBLANES, LANES), jnp.float32)] + [block] * (outs - 1),
        in_specs=[vmem] * 5 + [any_place] + [vmem] * parties,
        out_specs=[vmem] * outs,
        scratch_shapes=[
            pltpu.VMEM((tokens, breadth), jnp.bfloat16),
            pltpu.VMEM((height, breadth), jnp.float32),
            pltpu.VMEM((height, breadth), jnp.float32),
        ]
        + gather_scratch(outs - 1),
        compiler_params=pltpu.CompilerParams(vmem_limit_bytes=LIMIT),
        name="sketch",
    )(
        turned,
        sign_matrix,
        other_turned,
        other_signs,
        index_rows,
        rows,
        *[chunks[d] for d in range(parties)],
    )
    total = pl.pallas_call(
        functools.partial(own_kernel, parties, scale),
        out_shape=block,
        in_specs=[vmem, vmem, any_place],
        out_specs=vmem,
        scratch_shapes=gather_scratch(1),
        compiler_params=pltpu.CompilerParams(vmem_limit_bytes=LIMIT),
        cost_estimate=pl.CostEstimate(flops=0, bytes_accessed=8 * height * breadth, transcendentals=0),
        name="own",
    )(table, index_rows, rows)

    for out in range(1, outs):
        total = total + flipped(sums[out - 1], "param", 2 * out)
    return total.reshape(1, samples // parties)


def solution(mesh):
    in_specs = (P("ex", None, "param"), P("ex", "param", None), P("param"), P())
    out_specs = P("ex", "param")
    return jax.shard_map(
        on_device, mesh=mesh, in_specs=in_specs, out_specs=out_specs, check_vma=False
    )
```
